512 devices in a mesh: dp: 32 (over z_lo, y), label: 16 (over z_hi, x, core).
Axes of the slice: x: 4, y: 4, z: 16 (z_hi: 2, z_lo: 8; z = z_hi * 8 + z_lo), core: 2. Of those that a mesh axis runs over, the one named last changes fastest.
Arguments:
- features: bfloat16 [4096, 768], P('dp', 'label')
- label_ids: int32 [4096, 32], P('dp'), may hold values from 0 to 131071
- label_count: int32 [4096], P('dp'), may hold values from 1 to 32
- weight: float32 [131072, 768], P(('dp', 'label'))
- moment: float32 [131072, 768], P(('dp', 'label')), may hold values from -1.9073486e-05 to 1.9073486e-05
- second: float32 [131072, 768], P(('dp', 'label')), may hold values from 1e-13 to 1e-11
Outputs:
- lamb_step: float32 [131072, 768], P(('dp', 'label'))
- new_moment: float32 [131072, 768], P(('dp', 'label'))
- new_second: float32 [131072, 768], P(('dp', 'label'))
The draws below stay inside these ranges and needn't reach their ends.
All inputs are finite; a program needn't handle non-finite values.
Results may differ from the reference program's by a relative error of at most 0.0017.
Values may be sent and summed in bfloat16 or wider, within the bound.
A program may use at most 64 MiB of HBM per device.

```python
import math
import jax
import jax.numpy as jnp
from jax import lax

D = 768
ROWS_DEV = 256
IDS_MAX = 32
STEP = 10
QUERIES = 4096
LABELS = 131072


def shared_direction(key):
    return jax.random.normal(jax.random.fold_in(key, 5), (D,), jnp.float32)


def draw_features(key, part):
    direction = shared_direction(key)
    key = jax.random.fold_in(key, 7)
    pattern = jax.random.normal(key, (QUERIES, D), jnp.float32)
    return (pattern + 0.3 * direction[None, :]).astype(jnp.bfloat16)


def draw_weight(key, part):
    direction = shared_direction(key)
    key = jax.random.fold_in(key, 11)
    key_main, key_row, key_col = jax.random.split(key, 3)
    row_pos = jnp.arange(LABELS, dtype=jnp.float32) / LABELS
    row_scale = jnp.exp(jnp.log(4.0) * (row_pos - 0.5)) * jnp.exp(jnp.log(10.0) * (jax.random.uniform(key_row, (LABELS,), jnp.float32) - 0.5))
    col_scale = jnp.exp(jnp.log(10.0) * (jax.random.uniform(key_col, (D,), jnp.float32) - 0.5))
    pattern = jax.random.normal(key_main, (LABELS, D), jnp.float32)
    spread_part = 0.3 * pattern * row_scale[:, None] * col_scale[None, :]
    aligned = 20.0 / D ** 0.5 * direction[None, :]
    return (spread_part - aligned).astype(jnp.float32)


def set_ends(drawn, own_key, low, high):
    spot = [jax.random.randint(jax.random.fold_in(own_key, axis), (), 0, length) for axis, length in enumerate(drawn.shape)]
    widest = drawn.shape.index(max(drawn.shape))
    neighbour = spot[:widest] + [(spot[widest] + 1) % drawn.shape[widest]] + spot[widest + 1:]
    return drawn.at[tuple(spot)].set(low).at[tuple(neighbour)].set(high)


def block_levels(rng, extent, pieces, low, largest):
    gain = 1.0
    for axis_at, parts in pieces:
        draws = jax.random.uniform(jax.random.fold_in(jax.random.fold_in(rng, 6), axis_at), (parts,), jnp.float32, low / len(pieces), largest / len(pieces))
        gain = gain * jnp.repeat(jnp.exp(draws), extent[axis_at] // parts).reshape((-1,) + (1,) * (len(extent) - 1 - axis_at))
    return gain


def centred(own_key, extent, spread, most, pieces=(), kind=jnp.bfloat16):
    loudness = block_levels(own_key, extent, pieces, -0.22, 0.18) if pieces else 1.0
    array = jax.random.normal(own_key, extent, jnp.float32) * spread * loudness
    return jnp.minimum(jnp.maximum(array, -most), most).astype(kind)


def setup_inputs(seed: int = 0) -> dict:
    splits = jax.random.split(jax.random.key(seed), 7)
    features = draw_features(jax.random.fold_in(splits[6], 71), 0)
    label_ids = set_ends(jax.random.randint(splits[1], (QUERIES, IDS_MAX), 0, LABELS), jax.random.fold_in(splits[1], 1), 0, LABELS - 1).astype(jnp.int32)
    label_count = set_ends(jax.random.randint(splits[2], (QUERIES,), 1, IDS_MAX + 1), jax.random.fold_in(splits[2], 1), 1, IDS_MAX).astype(jnp.int32)
    weight = draw_weight(jax.random.fold_in(splits[6], 71), 0)
    moment = centred(splits[4], (LABELS, D), 0.000003, 1.9073486328125e-05, ((0, 512),), jnp.float32)
    second = jnp.clip(jnp.exp(math.log(9.999999960041972e-12) - 4.6051702 * jax.random.uniform(splits[5], (LABELS, D), jnp.float32) ** block_levels(splits[5], (LABELS, D), ((0, 512),), -0.2, 0.2)), 9.9999998245167e-14, 9.999999960041972e-12)
    return dict(features=features, label_ids=label_ids, label_count=label_count, weight=weight, moment=moment, second=second)


def block_grad(features, label_ids, label_count, weight_bf, start):
    total = features.shape[0]
    scale = 1.0 / D ** 0.5
    block = lax.dynamic_slice_in_dim(weight_bf, start, ROWS_DEV, 0)
    scores = lax.dot_general(features, block, (((1,), (1,)), ((), ())), preferred_element_type=jnp.float32) * scale
    slot_ok = lax.iota(jnp.int32, IDS_MAX)[None, :] < label_count[:, None]
    local = jnp.where(slot_ok, label_ids - start, -1).astype(jnp.int32)
    columns = lax.iota(jnp.int32, ROWS_DEV)
    targets = jnp.any(local[:, :, None] == columns[None, None, :], axis=1).astype(jnp.float32)
    dscore = ((jax.nn.sigmoid(scores) - targets) / total).astype(jnp.bfloat16)
    return lax.dot_general(dscore, features, (((0,), (0,)), ((), ())), preferred_element_type=jnp.float32) * scale

def reference(features, label_ids, label_count, weight, moment, second):
    weight_bf = weight.astype(jnp.bfloat16)
    starts = (jnp.arange(LABELS // ROWS_DEV) * ROWS_DEV).astype(jnp.int32)
    grads = lax.map(lambda start: block_grad(features, label_ids, label_count, weight_bf, start), starts)
    grad = grads.reshape(LABELS, D)
    new_moment = 0.9 * moment + 0.1 * grad
    new_second = 0.999 * second + 0.001 * grad * grad
    update = new_moment / (1.0 - 0.9 ** STEP) / (jnp.sqrt(new_second / (1.0 - 0.999 ** STEP)) + 1e-06) + 0.01 * weight
    trust = jnp.sqrt(jnp.sum(weight * weight)) / (jnp.sqrt(jnp.sum(update * update)) + 1e-06)
    return (trust * update, new_moment, new_second)
```

```python
import functools

import jax
import jax.numpy as jnp
from jax import lax
from jax.experimental import pallas as pl
from jax.experimental.pallas import tpu as pltpu
from jax.sharding import PartitionSpec as P

STEP = 10
MESH = pl.DeviceIdType.MESH
NX, NY, NZ = 4, 4, 16
WIDTH, ROWS, QUERIES = 768, 256, 4096
HALF = WIDTH // 2
BLOCK_D, BLOCK_Q = 48, 128
SCALE = 1.0 / WIDTH**0.5

GROUPS = {
    "own": (0, 1, "y"),
    "near_up": (1, 4, "x"),
    "near_down": (13, 16, "y"),
    "mid_up": (4, 7, "x"),
    "mid_down": (10, 13, "y"),
    "far_up": (7, 9, "x"),
    "far_down": (9, 10, "y"),
}


class Sems:
    def __init__(self, send, recv):
        self.send, self.recv, self.used = send, recv, 0

    def next(self):
        self.used += 1
        return self.send.at[self.used - 1], self.recv.at[self.used - 1]


N_SEMS = 180


def kernel(
    features, ids, count, weight, moment, second,
    update_out, moment_out, second_out, trust_out,
    feat_in, ids_in, ids_t, w_in, mom_in, sec_in, w_bf, held, labels, words, acc, sums,
    send, recv, local,
):
    dp, lb = lax.axis_index("dp"), lax.axis_index("label")
    x, y, core = lax.rem(lb // 2, NX), lax.rem(dp, NY), lax.rem(lb, 2)
    z = (lb // 8) * 8 + dp // NY

    def device(x, y, z, core):
        return {"dp": lax.rem(z, 8) * NY + y, "label": (z // 8) * 8 + x * 2 + core}

    def along(axis, by):
        if axis == "x":
            return device(lax.rem(x + by, NX), y, z, core)
        if axis == "y":
            return device(x, lax.rem(y + by, NY), z, core)
        if axis == "z":
            return device(x, y, lax.rem(z + by + NZ, NZ), core)
        return device(x, y, z, 1 - core)

    barrier = pltpu.get_barrier_semaphore()
    partners = [("x", i) for i in range(1, NX)] + [("y", i) for i in range(1, NY)]
    partners += [("z", i) for i in range(1, NZ)] + [("core", 1)]
    for axis, by in partners:
        pl.semaphore_signal(barrier, inc=1, device_id=along(axis, by), device_id_type=MESH)

    loads = []
    for i, (src, dst) in enumerate(
        [(features, feat_in), (ids, ids_in), (weight, w_in), (moment, mom_in), (second, sec_in)]
    ):
        loads.append(pltpu.make_async_copy(src, dst, local.at[i]))
        loads[-1].start()

    loads[0].wait()
    held[0, y, x, core] = jnp.transpose(feat_in[...].astype(jnp.float32)).astype(jnp.bfloat16)
    loads[1].wait()
    slots = jnp.transpose(ids_in[...])
    used = lax.broadcasted_iota(jnp.int32, slots.shape, 0) < count[...]
    ids_t[...] = jnp.where(used, slots, -1).reshape(4, 8, BLOCK_Q)
    labels[3, y, x] = ids_t[x]

    sems = Sems(send, recv)
    sent = []

    def copy(src, dst, to, pair=None):
        pair = sems.next() if pair is None else pair
        c = pltpu.make_async_remote_copy(src, dst, *pair, device_id=to, device_id_type=MESH)
        sent.append(c)
        c.start()
        return c

    pl.semaphore_wait(barrier, len(partners))

    z_recv = {name: sems.next()[1] for name in GROUPS if name != "own"}
    for d in [1, 15, 2, 14, 3, 13, 4, 12, 5, 11, 6, 10, 7, 9, 8]:
        there = NZ - d
        name = next(n for n, (a, b, _) in GROUPS.items() if a <= there < b)
        copy(
            held.at[0, y, x, core], held.at[there, y, x, core], along("z", d),
            (sems.next()[0], z_recv[name]),
        )

    toward = 1 - 2 * core
    label_recv = sems.next()[1]
    for k in range(4):
        to = device(x, y, lax.rem(z + toward * (k + 1) + NZ, NZ), core)
        there = 4 if k == 3 else (2 - k) * (1 - core) + (5 + k) * core
        copy(labels.at[3, y, x], labels.at[there, y, x], to, (sems.next()[0], label_recv))

    def wait_z(name):
        a, b, _ = GROUPS[name]
        part = held.at[a:b, y, x, core]
        pltpu.make_async_remote_copy(
            part, part, send.at[0], z_recv[name], device_id=along("z", 1), device_id_type=MESH
        ).wait_recv()

    first_hop, second_hop, cross = {}, {}, {}

    def hop1(name):
        a, b, axis = GROUPS[name]
        if name != "own":
            wait_z(name)
        part = held.at[a:b, y, x, core]
        first_hop[name] = [copy(part, part, along(axis, i)) for i in (1, 3, 2)]

    def line(name, at):
        a, b, axis = GROUPS[name]
        if axis == "x":
            return held.at[a:b, at, :, core]
        return held.at[a:b, :, at, core]

    def hop2(name):
        axis = GROUPS[name][2]
        other, mine, n = ("y", y, NY) if axis == "x" else ("x", x, NX)
        for c in first_hop[name]:
            c.wait_recv()
        part = line(name, mine)
        second_hop[name] = [copy(part, part, along(other, i)) for i in (1, 3, 2)]
        cross[name] = [copy(part, part, along("core", 1))]

    def hop3(name):
        axis = GROUPS[name][2]
        mine, n = (y, NY) if axis == "x" else (x, NX)
        for c, i in zip(second_hop[name], (1, 3, 2), strict=True):
            c.wait_recv()
            part = line(name, lax.rem(mine - i + n, n))
            cross[name].append(copy(part, part, along("core", 1)))

    def done(name):
        for c in cross[name]:
            c.wait_recv()

    hop1("own")
    loads[2].wait()
    w_bf[0] = w_in[:, :HALF].astype(jnp.bfloat16)
    w_bf[1] = w_in[:, HALF:].astype(jnp.bfloat16)
    acc[...] = jnp.zeros_like(acc)

    hop1("near_up")
    hop1("near_down")
    hop2("own")
    part = labels.at[pl.ds(3 * core, 5), y, x]
    everything = labels.at[0:4, y, x]
    pltpu.make_async_remote_copy(
        everything, everything, send.at[0], label_recv, device_id=along("z", 1), device_id_type=MESH
    ).wait_recv()
    label_x = [copy(part, part, along("x", i)) for i in (1, 3, 2)]
    hop1("mid_up")
    hop1("mid_down")
    hop2("near_up")
    hop2("near_down")
    for c in label_x:
        c.wait_recv()
    part = labels.at[pl.ds(3 * core, 5), y]
    label_y = [copy(part, part, along("y", i)) for i in (1, 3, 2)]
    hop3("own")
    hop1("far_up")
    hop1("far_down")
    hop2("mid_up")
    hop2("mid_down")
    for c in label_y:
        c.wait_recv()
    part = labels.at[pl.ds(5 * core, 3)]
    label_core = copy(part, part, along("core", 1))
    hop3("near_up")
    hop3("near_down")
    hop2("far_up")
    hop2("far_down")

    label_core.wait_recv()
    first = (dp * 16 + lb) * ROWS

    def mark(i, _):
        pos, at = i // NY, lax.rem(i, NY)
        pair = jnp.where(pos < 3, pos + 5, jnp.where(pos == 3, 0, jnp.where(pos == 4, 4, pos - 4)))
        local_id = labels[pos, at] - first
        word = local_id >> 5
        bit = jnp.left_shift(jnp.int32(1), local_id & 31)
        rows = lax.broadcasted_iota(jnp.int32, (8, BLOCK_Q), 0)
        out = jnp.zeros((8, BLOCK_Q), jnp.int32)
        for w in range(8):
            hit = jnp.where(word == w, bit, 0)
            hit = (hit[0] | hit[1]) | (hit[2] | hit[3])
            for by in (4, 2, 1):
                hit = hit | pltpu.roll(hit, by, 0)
            out = jnp.where(rows == w, hit, out)
        words[pair, at] = out
        return 0

    lax.fori_loop(0, 8 * NY, mark, 0)

    def pair(r, _):
        r = lax.rem(r, 8)
        lo = lax.rem(z + r, NZ) // 8
        q = NY * BLOCK_Q

        def slab(at):
            return jnp.concatenate([held[at, i].reshape(HALF, BLOCK_Q) for i in range(NY)], axis=1)

        near, far = slab(r), slab(r + 8)
        scores = jnp.dot(w_bf[lo], near, preferred_element_type=jnp.float32)
        scores += jnp.dot(w_bf[1 - lo], far, preferred_element_type=jnp.float32)
        prob = jax.nn.sigmoid(scores * SCALE)
        marks = jnp.concatenate([words[r, i] for i in range(NY)], axis=1)
        rows = lax.broadcasted_iota(jnp.int32, (32, q), 0)
        bits = jnp.left_shift(jnp.int32(1), rows)
        target = jnp.concatenate(
            [(jnp.broadcast_to(marks[w : w + 1], (32, q)) & bits) != 0 for w in range(8)], axis=0
        )
        dscore = ((prob - jnp.where(target, 1.0, 0.0)) * (1.0 / QUERIES)).astype(jnp.bfloat16)
        dims = (((1,), (1,)), ((), ()))
        acc[lo] += lax.dot_general(dscore, near, dims, preferred_element_type=jnp.float32)
        acc[1 - lo] += lax.dot_general(dscore, far, dims, preferred_element_type=jnp.float32)
        return 0

    hop3("mid_up")
    hop3("mid_down")
    for name in ("own", "near_up", "near_down", "mid_up", "mid_down"):
        done(name)
    lax.fori_loop(2, 7, pair, 0)
    hop3("far_up")
    hop3("far_down")
    done("far_up")
    done("far_down")
    lax.fori_loop(7, 10, pair, 0)

    loads[3].wait()
    loads[4].wait()
    step_rows = 32

    def refresh(i, carry):
        at = pl.ds(pl.multiple_of(i * step_rows, step_rows), step_rows)
        totals = list(carry)
        for h in range(2):
            cols = slice(h * HALF, (h + 1) * HALF)
            g = acc[h, at] * SCALE
            w = w_in[at, cols]
            m = 0.9 * mom_in[at, cols] + 0.1 * g
            v = 0.999 * sec_in[at, cols] + 0.001 * g * g
            u = (m * (1.0 / (1.0 - 0.9**STEP))) / (
                jnp.sqrt(v * (1.0 / (1.0 - 0.999**STEP))) + 1e-06
            ) + 0.01 * w
            update_out[at, cols] = u
            moment_out[at, cols] = m
            second_out[at, cols] = v
            for k, s in enumerate((w * w, u * u)):
                s = jnp.sum(s.reshape(step_rows // 8, 8, HALF), axis=0)
                totals[k] += s[:, :128] + s[:, 128:256] + s[:, 256:]
        return tuple(totals)

    zero = jnp.zeros((8, 128), jnp.float32)
    totals = lax.fori_loop(0, ROWS // step_rows, refresh, (zero, zero))
    value = jnp.concatenate([jnp.sum(t, axis=0, keepdims=True) for t in totals], axis=0)

    base = 4
    for stage, (axis, n) in enumerate((("core", 2), ("x", NX), ("y", NY), ("z", NZ))):
        sums[stage] = value
        order = sorted(range(1, n), key=lambda d: -min(d, n - d))
        cs = [copy(sums.at[stage], sums.at[base + d - 1], along(axis, d)) for d in order]
        for c in cs:
            c.wait_recv()
        for d in range(1, n):
            value = value + sums[base + d - 1]
        base += n - 1
    norms = jnp.sqrt(jnp.sum(value, axis=1, keepdims=True))
    trust = norms[0:1] / (norms[1:2] + 1e-06)
    trust_out[...] = jnp.broadcast_to(trust, trust_out.shape)

    for c in sent:
        c.wait_send()


def shards(features, label_ids, label_count, weight, moment, second):
    anywhere = pl.BlockSpec(memory_space=pl.ANY)
    vmem = pl.BlockSpec(memory_space=pltpu.VMEM)
    f32, bf16, i32 = jnp.float32, jnp.bfloat16, jnp.int32
    block = jax.ShapeDtypeStruct(weight.shape, f32)
    update, new_moment, new_second, trust = pl.pallas_call(
        kernel,
        name="step",
        out_shape=(block, block, block, jax.ShapeDtypeStruct((8, 128), f32)),
        in_specs=[anywhere, anywhere, vmem, anywhere, anywhere, anywhere],
        out_specs=(vmem, vmem, vmem, vmem),
        scratch_shapes=[
            pltpu.VMEM(features.shape, bf16),
            pltpu.VMEM(label_ids.shape, i32),
            pltpu.VMEM((4, 8, BLOCK_Q), i32),
            pltpu.VMEM(weight.shape, f32),
            pltpu.VMEM(weight.shape, f32),
            pltpu.VMEM(weight.shape, f32),
            pltpu.VMEM((2, ROWS, HALF), bf16),
            pltpu.VMEM((NZ, NY, NX, 2, BLOCK_D, BLOCK_Q), bf16),
            pltpu.VMEM((8, NY, NX, 8, BLOCK_Q), i32),
            pltpu.VMEM((8, NY, 8, BLOCK_Q), i32),
            pltpu.VMEM((2, ROWS, HALF), f32),
            pltpu.VMEM((26, 2, 128), f32),
            pltpu.SemaphoreType.DMA((N_SEMS,)),
            pltpu.SemaphoreType.DMA((N_SEMS,)),
            pltpu.SemaphoreType.DMA((5,)),
        ],
        compiler_params=pltpu.CompilerParams(
            collective_id=0, has_side_effects=True, vmem_limit_bytes=40 << 20
        ),
    )(features, label_ids, label_count.reshape(1, -1), weight, moment, second)
    return (trust[0, 0] * update, new_moment, new_second)


def solution(mesh):
    in_specs = (
        P("dp", "label"),
        P("dp", None),
        P("dp"),
        P(("dp", "label"), None),
        P(("dp", "label"), None),
        P(("dp", "label"), None),
    )
    out_specs = (P(("dp", "label"), None), P(("dp", "label"), None), P(("dp", "label"), None))
    return jax.shard_map(shards, mesh=mesh, in_specs=in_specs, out_specs=out_specs, check_vma=False)
```

```python
import jax
import jax.numpy as jnp
from jax import lax
from jax.experimental import pallas as pl
from jax.experimental.pallas import tpu as pltpu
from jax.sharding import PartitionSpec as P

STEP = 10
MESH = pl.DeviceIdType.MESH
NX, NY, NZ = 4, 4, 16
WIDTH, ROWS, QUERIES = 768, 256, 4096
HALF = WIDTH // 2
BLOCK_D, BLOCK_Q = 48, 128
SCALE = 1.0 / WIDTH**0.5
LOG2_E = 1.4426950408889634
N_SEMS = 220

GROUPS = {
    "own": (0, 1, "y"),
    "4": (4, 5, "x"),
    "12": (12, 13, "y"),
    "5": (5, 6, "x"),
    "11": (11, 12, "y"),
    "6": (6, 7, "x"),
    "10": (10, 11, "y"),
    "78": (7, 9, "x"),
    "9": (9, 10, "y"),
}
LAST = ("5", "11")
Z_ORDER = (8, 7, 9, 4, 12, 6, 10, 5, 11)
OTHERS = (1, 3, 2)
Z_FAR_FIRST = (8, 7, 9, 6, 10, 5, 11, 4, 12, 3, 13, 2, 14, 1, 15)
PLANE = sorted(
    ((i, j, k) for i in range(NX) for j in range(NY) for k in range(2) if i or j or k),
    key=lambda o: -(min(o[0], NX - o[0]) + min(o[1], NY - o[1]) + o[2]),
)


def kernel(
    features, ids, count, weight, moment, second,
    update_out, moment_out, second_out, trust_out,
    feat_in, ids_in, ids_t, w_in, mom_in, sec_in, w_bf, held, labels, words, acc, sums,
    send, recv, local,
):
    dp, lb = lax.axis_index("dp"), lax.axis_index("label")
    x, y, core = lax.rem(lb // 2, NX), lax.rem(dp, NY), lax.rem(lb, 2)
    z = (lb // 8) * 8 + dp // NY

    def device(x, y, z, core):
        return {"dp": lax.rem(z, 8) * NY + y, "label": (z // 8) * 8 + x * 2 + core}

    def along(axis, by):
        if axis == "x":
            return device(lax.rem(x + by, NX), y, z, core)
        if axis == "y":
            return device(x, lax.rem(y + by, NY), z, core)
        if axis == "z":
            return device(x, y, lax.rem(z + by, NZ), core)
        return device(x, y, z, 1 - core)

    def in_plane(offset):
        i, j, k = offset
        return device(lax.rem(x + i, NX), lax.rem(y + j, NY), z, lax.rem(core + k, 2))

    barrier = pltpu.get_barrier_semaphore()
    for by in Z_FAR_FIRST:
        pl.semaphore_signal(barrier, inc=1, device_id=along("z", by), device_id_type=MESH)
    for offset in PLANE:
        pl.semaphore_signal(barrier, inc=1, device_id=in_plane(offset), device_id_type=MESH)

    loads = []
    for i, (src, dst) in enumerate(
        [(features, feat_in), (ids, ids_in), (weight, w_in), (moment, mom_in), (second, sec_in)]
    ):
        loads.append(pltpu.make_async_copy(src, dst, local.at[i]))
        loads[-1].start()

    loads[0].wait()
    held[0, y, x, core] = feat_in[...]
    loads[1].wait()
    used = lax.broadcasted_iota(jnp.int32, ids_in.shape, 0) < count[...]
    ids_t[...] = jnp.where(used, ids_in[...], -1).reshape(4, 8, BLOCK_Q)
    row, col = jnp.where(core == 0, y, x), jnp.where(core == 0, x, y)
    labels[3 + 5 * core, row, col] = ids_t[x]
    loads[2].wait()
    w_bf[0] = w_in[:, :HALF].astype(jnp.bfloat16)
    w_bf[1] = w_in[:, HALF:].astype(jnp.bfloat16)
    acc[...] = jnp.zeros_like(acc)

    used_sems, sent = [0], []

    def sems():
        used_sems[0] += 1
        return send.at[used_sems[0] - 1], recv.at[used_sems[0] - 1]

    def copy(src, dst, to, recv_sem=None):
        s, r = sems()
        c = pltpu.make_async_remote_copy(
            src, dst, s, r if recv_sem is None else recv_sem, device_id=to, device_id_type=MESH
        )
        sent.append(c)
        c.start()
        return c

    def arrived(part, sem):
        pltpu.make_async_remote_copy(
            part, part, send.at[0], sem, device_id=along("z", 1), device_id_type=MESH
        ).wait_recv()

    pl.semaphore_wait(barrier, len(Z_FAR_FIRST) + len(PLANE))

    toward = 1 - 2 * core
    label_z = sems()[1]
    for k in (3, 2, 1, 0):
        to = device(x, y, lax.rem(z + toward * (k + 1) + NZ, NZ), core)
        there = 8 - core if k == 3 else (2 - k) * (1 - core) + (4 + k) * core
        copy(ids_t.at[x], labels.at[there, row, col], to, label_z)

    def label_hop(first, i):
        on_x = (core == 0) == first
        return device(
            jnp.where(on_x, lax.rem(x + i, NX), x), jnp.where(on_x, y, lax.rem(y + i, NY)), z, core
        )

    z_recv = {name: sems()[1] for name in GROUPS if name != "own"}
    for d in Z_ORDER:
        there = NZ - d
        name = next(n for n, (a, b, _) in GROUPS.items() if a <= there < b)
        copy(held.at[0, y, x, core], held.at[there, y, x, core], along("z", d), z_recv[name])

    hops, cross = {}, {}

    def hop1(name):
        a, b, axis = GROUPS[name]
        part = held.at[a:b, y, x, core]
        if name != "own":
            arrived(part, z_recv[name])
        hops[name] = [copy(part, part, along(axis, i)) for i in OTHERS]

    def line(name, at):
        a, b, axis = GROUPS[name]
        return held.at[a:b, at, :, core] if axis == "x" else held.at[a:b, :, at, core]

    def to_core(name, part):
        cross.setdefault(name, []).append(copy(part, part, along("core", 1)))

    passed = [[], [], []]

    def to_z(k, at):
        ups = held.at[(NZ - k) % NZ, :, at, core], held.at[NZ - 1 - k, :, at, core]
        downs = held.at[k, :, at, core], held.at[k + 1, :, at, core]
        passed[k].append((copy(*ups, along("z", 1)), copy(*downs, along("z", NZ - 1))))

    def from_z(k, n):
        at = lax.rem(x + 4 - (0, *OTHERS)[n], 4)
        for c in passed[k][n]:
            c.wait_recv()
        if k < 2:
            to_z(k + 1, at)
        for r in (k + 1, NZ - 1 - k):
            if k == 2:
                to_core("z3", held.at[r, :, at, core])
            elif n == 3:
                to_core("z" + str(k + 1), held.at[r, :, :, core])

    def hop2(name):
        other, mine = ("y", y) if GROUPS[name][2] == "x" else ("x", x)
        for c in hops[name]:
            c.wait_recv()
        part = line(name, mine)
        hops[name] = [copy(part, part, along(other, i)) for i in OTHERS]
        if name == "own":
            to_z(0, mine)
        if name in LAST:
            to_core(name, part)

    def hop3(name):
        a, b, axis = GROUPS[name]
        mine = y if axis == "x" else x
        for c, i in zip(hops[name], OTHERS, strict=True):
            c.wait_recv()
            at = lax.rem(mine + 4 - i, 4)
            if name == "own":
                to_z(0, at)
            if name in LAST:
                to_core(name, line(name, at))
        if name not in LAST:
            for r in range(a, b):
                to_core(name, held.at[r, :, :, core])

    def done(name):
        for c in cross[name]:
            c.wait_recv()

    def label_send(part, to):
        return [copy(part, part, d) for d in to]

    hop1("own")
    hop2("own")
    arrived(labels.at[0:4, row, col], label_z)
    part = labels.at[pl.ds(4 * core, 4), row, col]
    label_sent = label_send(part, [label_hop(True, i) for i in OTHERS])
    hop1("4")
    hop1("12")
    hop3("own")
    hop1("5")
    hop1("11")
    hop1("6")
    hop1("10")
    hop1("78")
    hop1("9")
    hop2("4")
    hop2("12")
    for c in label_sent:
        c.wait_recv()
    part = labels.at[pl.ds(4 * core, 4), row]
    label_sent = label_send(part, [label_hop(False, i) for i in OTHERS])
    from_z(0, 0)
    from_z(0, 1)
    hop2("6")
    hop2("10")
    from_z(0, 2)
    from_z(0, 3)
    hop2("78")
    hop2("9")
    hop2("5")
    hop2("11")
    for c in label_sent:
        c.wait_recv()
    label_sent = []
    for i in range(2):
        label_sent += label_send(labels.at[pl.ds(4 * core + 2 * i, 2)], [along("core", 1)])
    from_z(1, 0)
    from_z(1, 1)
    hop3("4")
    hop3("12")

    for c in label_sent:
        c.wait_recv()
    first = (dp * 16 + lb) * ROWS

    def mark(i, core):
        pos, at = i // NY, lax.rem(i, NY)
        if core == 0:
            pair, found = lax.rem(pos + 5, 8), labels[pos, at]
        else:
            pair, found = pos + 1, labels[4 + pos, :, at]
        local_id = found - first
        word = local_id >> 5
        bit = jnp.left_shift(jnp.int32(1), local_id & 31)
        rows = lax.broadcasted_iota(jnp.int32, (8, BLOCK_Q), 0)
        out = jnp.zeros((8, BLOCK_Q), jnp.int32)
        for w in range(8):
            hit = jnp.where(word == w, bit, 0)
            hit = (hit[0] | hit[1]) | (hit[2] | hit[3])
            for by in (4, 2, 1):
                hit = hit | pltpu.roll(hit, by, 0)
            out = jnp.where(rows == w, hit, out)
        words[pair, at] = out
        return core

    for i in range(2):
        lax.fori_loop(0, 4 * NY, lambda n, _, i=i: (mark(n, i), 0)[1], 0)

    def pair(r):
        lo = lax.rem(z + r, NZ) // 8
        q = NY * BLOCK_Q

        def slab(at):
            return jnp.concatenate([held[at, i].reshape(HALF, BLOCK_Q) for i in range(NY)], axis=1)

        near, far = slab(r), slab(r + 8)
        scores = jnp.dot(
            jnp.concatenate([w_bf[lo], w_bf[1 - lo]], axis=1),
            jnp.concatenate([near, far], axis=0),
            preferred_element_type=jnp.float32,
        )
        prob = 1.0 / (1.0 + jnp.exp2(scores * (-SCALE * LOG2_E)))
        marks = jnp.concatenate([words[r, i] for i in range(NY)], axis=1)
        bits = jnp.left_shift(jnp.int32(1), lax.broadcasted_iota(jnp.int32, (32, q), 0))
        target = jnp.concatenate(
            [(jnp.broadcast_to(marks[w : w + 1], (32, q)) & bits) != 0 for w in range(8)], axis=0
        )
        dscore = (prob - jnp.where(target, 1.0, 0.0)).astype(jnp.bfloat16)
        dims = (((1,), (1,)), ((), ()))
        acc[lo] += lax.dot_general(dscore, near, dims, preferred_element_type=jnp.float32)
        acc[1 - lo] += lax.dot_general(dscore, far, dims, preferred_element_type=jnp.float32)

    def pairs(first_r, by, n):
        def one(i, _):
            pair(lax.rem(first_r + i * by, 8))
            return 0

        lax.fori_loop(0, n, one, 0)

    from_z(1, 2)
    from_z(1, 3)
    done("4")
    done("12")
    pairs(4, 1, 1)
    hop3("6")
    hop3("10")
    done("6")
    done("10")
    done("z2")
    from_z(2, 0)
    pairs(2, 4, 2)
    hop3("78")
    hop3("9")
    from_z(2, 1)
    for name in ("own", "z1", "78", "9"):
        done(name)
    pairs(7, 1, 3)
    hop3("5")
    hop3("11")
    from_z(2, 2)
    from_z(2, 3)
    for name in ("z3", "5", "11"):
        done(name)
    pairs(3, 2, 2)

    loads[3].wait()
    loads[4].wait()
    step_rows = 32

    def refresh(i, carry):
        at = pl.ds(pl.multiple_of(i * step_rows, step_rows), step_rows)
        totals = list(carry)
        for h in range(2):
            cols = slice(h * HALF, (h + 1) * HALF)
            g = acc[h, at] * (SCALE / QUERIES)
            w = w_in[at, cols]
            m = 0.9 * mom_in[at, cols] + 0.1 * g
            v = 0.999 * sec_in[at, cols] + 0.001 * g * g
            u = (m * (1.0 / (1.0 - 0.9**STEP))) / (
                jnp.sqrt(v * (1.0 / (1.0 - 0.999**STEP))) + 1e-06
            ) + 0.01 * w
            update_out[at, cols] = u
            moment_out[at, cols] = m
            second_out[at, cols] = v
            for k, s in enumerate((w * w, u * u)):
                s = jnp.sum(s.reshape(step_rows // 8, 8, HALF), axis=0)
                totals[k] += s[:, :128] + s[:, 128:256] + s[:, 256:]
        return tuple(totals)

    zero = jnp.zeros((8, 128), jnp.float32)
    totals = lax.fori_loop(0, ROWS // step_rows, refresh, (zero, zero))
    value = jnp.concatenate([jnp.sum(t, axis=0, keepdims=True) for t in totals], axis=0)

    base = 2
    to_plane = [in_plane(o) for o in PLANE]
    to_column = [along("z", by) for by in Z_FAR_FIRST]
    for stage, to in enumerate((to_plane, to_column)):
        sums[stage] = value
        cs = [copy(sums.at[stage], sums.at[base + i], d) for i, d in enumerate(to)]
        for c in cs:
            c.wait_recv()
        value = value + jnp.sum(sums[base : base + len(to)], axis=0)
        base += len(to)
    norms = jnp.sqrt(jnp.sum(value, axis=1, keepdims=True))
    trust = norms[0:1] / (norms[1:2] + 1e-06)
    trust_out[...] = jnp.broadcast_to(trust, trust_out.shape)

    for c in sent:
        c.wait_send()


def finish(update, moment, second, trust, step_out, moment_out, second_out, scaled, done):
    copies = [
        pltpu.make_async_copy(moment, moment_out, done.at[0]),
        pltpu.make_async_copy(second, second_out, done.at[1]),
    ]
    for c in copies:
        c.start()
    n = ROWS // 4
    for i in range(4):
        at = pl.ds(i * n, n)
        scaled[at] = update[at] * trust[0:1, 0:1]
        copies.append(pltpu.make_async_copy(scaled.at[at], step_out.at[at], done.at[2 + i]))
        copies[-1].start()
    for c in copies:
        c.wait()


def shards(features, label_ids, label_count, weight, moment, second):
    hbm = pl.BlockSpec(memory_space=pltpu.HBM)
    vmem = pl.BlockSpec(memory_space=pltpu.VMEM)
    f32, bf16, i32 = jnp.float32, jnp.bfloat16, jnp.int32
    block = jax.ShapeDtypeStruct(weight.shape, f32)
    results = pl.pallas_call(
        kernel,
        name="step",
        out_shape=(block, block, block, jax.ShapeDtypeStruct((8, 128), f32)),
        in_specs=[hbm, hbm, vmem, hbm, hbm, hbm],
        out_specs=(vmem, vmem, vmem, vmem),
        scratch_shapes=[
            pltpu.VMEM(features.shape[::-1], bf16),
            pltpu.VMEM(label_ids.shape[::-1], i32),
            pltpu.VMEM((4, 8, BLOCK_Q), i32),
            pltpu.VMEM(weight.shape, f32),
            pltpu.VMEM(weight.shape, f32),
            pltpu.VMEM(weight.shape, f32),
            pltpu.VMEM((2, ROWS, HALF), bf16),
            pltpu.VMEM((NZ, NY, NX, 2, BLOCK_D, BLOCK_Q), bf16),
            pltpu.VMEM((9, NY, NX, 8, BLOCK_Q), i32),
            pltpu.VMEM((8, NY, 8, BLOCK_Q), i32),
            pltpu.VMEM((2, ROWS, HALF), f32),
            pltpu.VMEM((48, 2, 128), f32),
            pltpu.SemaphoreType.DMA((N_SEMS,)),
            pltpu.SemaphoreType.DMA((N_SEMS,)),
            pltpu.SemaphoreType.DMA((5,)),
        ],
        compiler_params=pltpu.CompilerParams(
            collective_id=0, has_side_effects=True, vmem_limit_bytes=411 << 17
        ),
    )(features.T, label_ids.T, label_count.reshape(1, -1), weight, moment, second)
    return pl.pallas_call(
        finish,
        name="finish",
        out_shape=(block, block, block),
        in_specs=[vmem] * 4,
        out_specs=(hbm, hbm, hbm),
        scratch_shapes=[pltpu.VMEM(weight.shape, f32), pltpu.SemaphoreType.DMA((6,))],
        compiler_params=pltpu.CompilerParams(vmem_limit_bytes=8 << 20),
    )(*results)


def solution(mesh):
    in_specs = (
        P("dp", "label"),
        P("dp", None),
        P("dp"),
        P(("dp", "label"), None),
        P(("dp", "label"), None),
        P(("dp", "label"), None),
    )
    out_specs = (P(("dp", "label"), None), P(("dp", "label"), None), P(("dp", "label"), None))
    return jax.shard_map(shards, mesh=mesh, in_specs=in_specs, out_specs=out_specs, check_vma=False)
```

```python
import jax
import jax.numpy as jnp
from jax import lax
from jax.experimental import pallas as pl
from jax.experimental.pallas import tpu as pltpu
from jax.sharding import PartitionSpec as P

STEP = 10
MESH = pl.DeviceIdType.MESH
NX, NY, NZ = 4, 4, 16
WIDTH, ROWS, QUERIES = 768, 256, 4096
HALF = WIDTH // 2
BLOCK_D, BLOCK_Q = 48, 128
SCALE = 1.0 / WIDTH**0.5
LOG2_E = 1.4426950408889634
N_SEMS = 230

GROUPS = {
    "own": (0, 1, "y"),
    "4": (4, 5, "x"),
    "12": (12, 13, "y"),
    "5": (5, 6, "x"),
    "11": (11, 12, "y"),
    "6": (6, 7, "x"),
    "10": (10, 11, "y"),
    "78": (7, 9, "x"),
    "9": (9, 10, "y"),
}
FORWARDED = ()
LAST = ("5", "11")
Z_ORDER = (5, 12, 9, 4, 7, 6, 11, 10, 8)
OTHERS = (1, 3, 2)
Z_FAR_FIRST = (8, 7, 9, 6, 10, 5, 11, 4, 12, 3, 13, 2, 14, 1, 15)
ROW = ((2, 1), (2, 0), (1, 1), (3, 1), (1, 0), (3, 0), (0, 1))

ORDER = (
    ("h1", "own"), ("h2", "own"), ("lab", 0), ("h1", "4"), ("lab", 1), ("h1", "12"), ("h3", "own"),
    ("h1", "11"), ("h1", "5"), ("h1", "10"), ("h1", "6"), ("h2", "4"), ("h1", "78"), ("h1", "9"),
    ("fz", 0, 0), ("h2", "12"), ("lab", 2), ("h2", "11"), ("h2", "5"), ("h2", "10"), ("h2", "6"),
    ("fz", 0, 1), ("fz", 0, 2), ("lab", 3), ("fz", 0, 3), ("fz", 1, 0), ("h2", "9"), ("h2", "78"),
    ("h3", "4"), ("fz", 1, 1), ("fz", 1, 2), ("h3", "12"), ("fz", 1, 3), ("fz", 2, 0), ("h3", "5"),
    ("h3", "6"), ("p", 4), ("fz", 2, 1), ("h3", "10"), ("h3", "11"), ("h3", "9"), ("p", 6),
    ("fz", 2, 2), ("fz", 2, 3), ("p", 2), ("h3", "78"), ("p", 1, 5, 3), ("p", 0, 7),
)


def kernel(
    features, ids, count, weight, moment, second,
    update_hbm, moment_hbm, second_hbm, trust_hbm,
    feat_in, ids_in, count_in, ids_t, w_in, mom_in, sec_in, w_bf, held, labels, words, acc, sums,
    update_out, moment_out, second_out, trust_out, send, recv, local,
):
    dp, lb = lax.axis_index("dp"), lax.axis_index("label")
    x, y, core = lax.rem(lb // 2, NX), lax.rem(dp, NY), lax.rem(lb, 2)
    z = (lb // 8) * 8 + dp // NY

    def device(x, y, z, core):
        return {"dp": lax.rem(z, 8) * NY + y, "label": (z // 8) * 8 + x * 2 + core}

    def along(axis, by):
        if axis == "x":
            return device(lax.rem(x + by, NX), y, z, core)
        if axis == "y":
            return device(x, lax.rem(y + by, NY), z, core)
        if axis == "z":
            return device(x, y, lax.rem(z + by, NZ), core)
        return device(x, y, z, 1 - core)

    def in_row(by, cores):
        return device(lax.rem(x + by, NX), y, z, lax.rem(core + cores, 2))

    loads = {}
    for i, (name, src, dst) in enumerate(
        [
            ("features", features, feat_in),
            ("ids", ids, ids_in),
            ("count", count, count_in),
            ("weight", weight, w_in),
            ("moment", moment, mom_in),
            ("second", second, sec_in),
        ]
    ):
        loads[name] = pltpu.make_async_copy(src, dst, local.at[i])
        loads[name].start()

    barrier = pltpu.get_barrier_semaphore()
    column = [along("z", by) for by in Z_FAR_FIRST]
    file = [along("y", by) for by in (2, 1, 3)]
    row_ = [in_row(*o) for o in ROW]
    greeted = column + file + row_
    for to in greeted:
        pl.semaphore_signal(barrier, inc=1, device_id=to, device_id_type=MESH)

    loads["features"].wait()
    held[0, y, x, core] = feat_in[...]
    loads["ids"].wait()
    loads["count"].wait()
    used = lax.broadcasted_iota(jnp.int32, ids_in.shape, 0) < count_in[...]
    ids_t[...] = jnp.where(used, ids_in[...], -1).reshape(4, 8, BLOCK_Q)
    row, col = jnp.where(core == 0, y, x), jnp.where(core == 0, x, y)
    labels[3 + 5 * core, row, col] = ids_t[x]

    used_sems, sent = [0], []

    def sems():
        used_sems[0] += 1
        return send.at[used_sems[0] - 1], recv.at[used_sems[0] - 1]

    def copy(src, dst, to, recv_sem=None):
        s, r = sems()
        c = pltpu.make_async_remote_copy(
            src, dst, s, r if recv_sem is None else recv_sem, device_id=to, device_id_type=MESH
        )
        sent.append(c)
        c.start()
        return c

    def arrived(part, sem):
        pltpu.make_async_remote_copy(
            part, part, send.at[0], sem, device_id=along("z", 1), device_id_type=MESH
        ).wait_recv()

    pl.semaphore_wait(barrier, len(greeted))

    toward = 1 - 2 * core
    label_z = sems()[1]
    for k in (3, 2, 1, 0):
        to = device(x, y, lax.rem(z + toward * (k + 1) + NZ, NZ), core)
        there = 8 - core if k == 3 else (2 - k) * (1 - core) + (4 + k) * core
        copy(ids_t.at[x], labels.at[there, row, col], to, label_z)

    def label_hop(first, i):
        on_x = (core == 0) == first
        return device(
            jnp.where(on_x, lax.rem(x + i, NX), x), jnp.where(on_x, y, lax.rem(y + i, NY)), z, core
        )

    z_recv = {name: sems()[1] for name in GROUPS if name != "own"}
    for d in Z_ORDER:
        there = NZ - d
        name = next(n for n, (a, b, _) in GROUPS.items() if a <= there < b)
        copy(held.at[0, y, x, core], held.at[there, y, x, core], along("z", d), z_recv[name])

    hops, cross = {}, {}

    def hop1(name):
        a, b, axis = GROUPS[name]
        part = held.at[a:b, y, x, core]
        if name != "own":
            arrived(part, z_recv[name])
        hops[name] = [copy(part, part, along(axis, i)) for i in OTHERS]

    def line(name, at, part=slice(0, 4)):
        a, b, axis = GROUPS[name]
        return held.at[a:b, at, part, core] if axis == "x" else held.at[a:b, part, at, core]

    def to_core(name, part):
        cross.setdefault(name, []).append(copy(part, part, along("core", 1)))

    passed = [[], [], []]

    def to_z(k, at):
        ups = held.at[(NZ - k) % NZ, :, at, core], held.at[NZ - 1 - k, :, at, core]
        downs = held.at[k, :, at, core], held.at[k + 1, :, at, core]
        passed[k].append((copy(*ups, along("z", 1)), copy(*downs, along("z", NZ - 1))))

    def from_z(k, n):
        at = lax.rem(x + 4 - (0, *OTHERS)[n], 4)
        for c in passed[k][n]:
            c.wait_recv()
        if k < 2:
            to_z(k + 1, at)
        for r in (k + 1, NZ - 1 - k):
            if k == 2:
                to_core("z3", held.at[r, :, at, core])
            elif n == 3:
                to_core("z" + str(k + 1), held.at[r, :, :, core])

    def hop2(name):
        other, mine = ("y", y) if GROUPS[name][2] == "x" else ("x", x)
        for c in hops[name]:
            c.wait_recv()
        part = line(name, mine)
        to = OTHERS[:2] if name in FORWARDED else OTHERS
        hops[name] = [copy(part, part, along(other, i)) for i in to]
        if name == "own":
            to_z(0, mine)
        if name in LAST:
            to_core(name, part)

    def forward(name):
        other, mine = ("y", y) if GROUPS[name][2] == "x" else ("x", x)
        halves = []
        for c, i in zip(hops[name], OTHERS[:2], strict=True):
            c.wait_recv()
            at = lax.rem(mine + 4 - i, 4)
            part = line(name, at, slice(0, 2) if i == 1 else slice(2, 4))
            halves.append(copy(part, part, along(other, i)))
            if name in LAST:
                to_core(name, line(name, at))
        hops[name] = halves

    def hop3(name):
        a, b, axis = GROUPS[name]
        mine = y if axis == "x" else x
        for c, i in zip(hops[name], OTHERS, strict=False):
            c.wait_recv()
            at = lax.rem(mine + 4 - i, 4)
            if name == "own":
                to_z(0, at)
            if name in LAST and name not in FORWARDED:
                to_core(name, line(name, at))
        if name not in LAST:
            for r in range(a, b):
                to_core(name, held.at[r, :, :, core])
        elif name in FORWARDED:
            to_core(name, line(name, lax.rem(mine + 2, 4)))

    waiting = set()

    def done(name):
        if name not in waiting:
            waiting.add(name)
            for c in cross[name]:
                c.wait_recv()

    def slot(r):
        found = [n for n, (a, b, _) in GROUPS.items() if a <= r < b]
        return found[0] if found else "z" + str(min(r, NZ - r))

    first = (dp * 16 + lb) * ROWS

    def mark(i, core):
        pos, at = i // NY, lax.rem(i, NY)
        if core == 0:
            pair, found = lax.rem(pos + 5, 8), labels[pos, at]
        else:
            pair, found = pos + 1, labels[4 + pos, :, at]
        local_id = found - first
        word = local_id >> 5
        bit = jnp.left_shift(jnp.int32(1), local_id & 31)
        rows = lax.broadcasted_iota(jnp.int32, (8, BLOCK_Q), 0)
        out = jnp.zeros((8, BLOCK_Q), jnp.int32)
        for w in range(8):
            hit = jnp.where(word == w, bit, 0)
            hit = (hit[0] | hit[1]) | (hit[2] | hit[3])
            for by in (4, 2, 1):
                hit = hit | pltpu.roll(hit, by, 0)
            out = jnp.where(rows == w, hit, out)
        words[pair, at] = out
        return core

    label_sent = []

    def label(stage):
        if stage == 0:
            arrived(labels.at[0:4, row, col], label_z)
        for c in label_sent:
            c.wait_recv()
        label_sent.clear()
        if stage == 0:
            part = labels.at[pl.ds(4 * core, 4), row, col]
            label_sent.extend(copy(part, part, label_hop(True, i)) for i in OTHERS)
        elif stage == 1:
            part = labels.at[pl.ds(4 * core, 4), row]
            label_sent.extend(copy(part, part, label_hop(False, i)) for i in OTHERS)
        elif stage == 2:
            part = labels.at[pl.ds(4 * core, 4)]
            label_sent.append(copy(part, part, along("core", 1)))
        else:
            for i in range(2):
                lax.fori_loop(0, 4 * NY, lambda n, _, i=i: (mark(n, i), 0)[1], 0)

    def pair(r):
        lo = lax.rem(z + r, NZ) // 8
        q = NY * BLOCK_Q

        def slab(at):
            return jnp.concatenate([held[at, i].reshape(HALF, BLOCK_Q) for i in range(NY)], axis=1)

        block = jnp.concatenate([slab(r), slab(r + 8)], axis=0)
        both = jnp.concatenate([w_bf[lo], w_bf[1 - lo]], axis=1)
        scores = jnp.dot(both, block, preferred_element_type=jnp.float32)
        prob = 1.0 / (1.0 + jnp.exp2(scores * (-SCALE * LOG2_E)))
        marks = jnp.concatenate([words[r, i] for i in range(NY)], axis=1)
        bits = jnp.left_shift(jnp.int32(1), lax.broadcasted_iota(jnp.int32, (32, q), 0))
        target = jnp.concatenate(
            [(jnp.broadcast_to(marks[w : w + 1], (32, q)) & bits) != 0 for w in range(8)], axis=0
        )
        dscore = (prob - jnp.where(target, 1.0, 0.0)).astype(jnp.bfloat16)
        dims = (((1,), (1,)), ((), ()))
        g = lax.dot_general(dscore, block, dims, preferred_element_type=jnp.float32)
        acc[lo] += g[:, :HALF]
        acc[1 - lo] += g[:, HALF:]

    steps = {"h1": hop1, "h2": hop2, "h2b": forward, "h3": hop3, "fz": from_z, "lab": label}
    for at, (what, *args) in enumerate(ORDER):
        if at == 2:
            loads["weight"].wait()
            w_bf[0] = w_in[:, :HALF].astype(jnp.bfloat16)
            w_bf[1] = w_in[:, HALF:].astype(jnp.bfloat16)
            acc[...] = jnp.zeros_like(acc)
        if what != "p":
            steps[what](*args)
            continue
        for r in args:
            done(slot(r))
            done(slot(r + 8))
        for r in args:
            pair(r)

    loads["moment"].wait()
    loads["second"].wait()
    step_rows = 32

    def refresh(i, carry):
        at = pl.ds(pl.multiple_of(i * step_rows, step_rows), step_rows)
        totals = list(carry)
        for h in range(2):
            cols = slice(h * HALF, (h + 1) * HALF)
            g = acc[h, at] * (SCALE / QUERIES)
            w = w_in[at, cols]
            m = 0.9 * mom_in[at, cols] + 0.1 * g
            v = 0.999 * sec_in[at, cols] + 0.001 * g * g
            u = (m * (1.0 / (1.0 - 0.9**STEP))) / (
                jnp.sqrt(v * (1.0 / (1.0 - 0.999**STEP))) + 1e-06
            ) + 0.01 * w
            update_out[at, cols] = u
            moment_out[at, cols] = m
            second_out[at, cols] = v
            for k, s in enumerate((w * w, u * u)):
                s = jnp.sum(s.reshape(step_rows // 8, 8, HALF), axis=0)
                totals[k] += s[:, :128] + s[:, 128:256] + s[:, 256:]
        return tuple(totals)

    zero = jnp.zeros((8, 128), jnp.float32)
    totals = lax.fori_loop(0, ROWS // step_rows, refresh, (zero, zero))
    stores = [
        pltpu.make_async_copy(update_out, update_hbm, local.at[6]),
        pltpu.make_async_copy(moment_out, moment_hbm, local.at[7]),
        pltpu.make_async_copy(second_out, second_hbm, local.at[8]),
    ]
    for c in stores:
        c.start()
    value = jnp.concatenate([jnp.sum(t, axis=0, keepdims=True) for t in totals], axis=0)

    base = 3
    for stage, to in enumerate((row_, file, column)):
        sums[stage] = value
        cs = [copy(sums.at[stage], sums.at[base + i], d) for i, d in enumerate(to)]
        for c in cs:
            c.wait_recv()
        value = value + jnp.sum(sums[base : base + len(to)], axis=0)
        base += len(to)
    norms = jnp.sqrt(jnp.sum(value, axis=1, keepdims=True))
    trust = norms[0:1] / (norms[1:2] + 1e-06)
    trust_out[...] = jnp.broadcast_to(trust, trust_out.shape)
    store = pltpu.make_async_copy(trust_out, trust_hbm, local.at[0])
    store.start()
    for c in sent:
        c.wait_send()
    for c in stores:
        c.wait()
    store.wait()


def finish(update, moment, second, trust, step_out, moment_out, second_out, held, scaled, by, given, done):
    parts, n = 4, ROWS // 4
    factor = pltpu.make_async_copy(trust, by, given.at[3, 0])
    factor.start()
    reads, writes = {}, []
    for i in range(parts):
        at = pl.ds(i * n, n)
        for k, src in enumerate((update, moment, second)):
            reads[k, i] = pltpu.make_async_copy(src.at[at], held.at[k, at], given.at[k, i])
            reads[k, i].start()
    factor.wait()
    for i in range(parts):
        at = pl.ds(i * n, n)
        for k, dst in enumerate((step_out, moment_out, second_out)):
            reads[k, i].wait()
            if k == 0:
                scaled[at] = held[0, at] * by[0:1, 0:1]
            src = scaled.at[at] if k == 0 else held.at[k, at]
            writes.append(pltpu.make_async_copy(src, dst.at[at], done.at[k, i]))
            writes[-1].start()
    for c in writes:
        c.wait()


def shards(features, label_ids, label_count, weight, moment, second):
    hbm = pl.BlockSpec(memory_space=pltpu.HBM)
    f32, bf16, i32 = jnp.float32, jnp.bfloat16, jnp.int32
    block = jax.ShapeDtypeStruct(weight.shape, f32)
    results = pl.pallas_call(
        kernel,
        name="step",
        out_shape=(block, block, block, jax.ShapeDtypeStruct((8, 128), f32)),
        in_specs=[hbm] * 6,
        out_specs=(hbm, hbm, hbm, hbm),
        scratch_shapes=[
            pltpu.VMEM(features.shape[::-1], bf16),
            pltpu.VMEM(label_ids.shape[::-1], i32),
            pltpu.VMEM((1, BLOCK_Q), i32),
            pltpu.VMEM((4, 8, BLOCK_Q), i32),
            pltpu.VMEM(weight.shape, f32),
            pltpu.VMEM(weight.shape, f32),
            pltpu.VMEM(weight.shape, f32),
            pltpu.VMEM((2, ROWS, HALF), bf16),
            pltpu.VMEM((NZ, NY, NX, 2, BLOCK_D, BLOCK_Q), bf16),
            pltpu.VMEM((9, NY, NX, 8, BLOCK_Q), i32),
            pltpu.VMEM((8, NY, 8, BLOCK_Q), i32),
            pltpu.VMEM((2, ROWS, HALF), f32),
            pltpu.VMEM((28, 2, 128), f32),
            pltpu.VMEM(weight.shape, f32),
            pltpu.VMEM(weight.shape, f32),
            pltpu.VMEM(weight.shape, f32),
            pltpu.VMEM((8, 128), f32),
            pltpu.SemaphoreType.DMA((N_SEMS,)),
            pltpu.SemaphoreType.DMA((N_SEMS,)),
            pltpu.SemaphoreType.DMA((9,)),
        ],
        compiler_params=pltpu.CompilerParams(
            collective_id=0, has_side_effects=True, vmem_limit_bytes=60 << 20
        ),
    )(features.T, label_ids.T, label_count.reshape(1, -1), weight, moment, second)
    return pl.pallas_call(
        finish,
        name="finish",
        out_shape=(block, block, block),
        in_specs=[hbm] * 4,
        out_specs=(hbm, hbm, hbm),
        scratch_shapes=[
            pltpu.VMEM((3, *weight.shape), f32),
            pltpu.VMEM(weight.shape, f32),
            pltpu.VMEM((8, 128), f32),
            pltpu.SemaphoreType.DMA((4, 4)),
            pltpu.SemaphoreType.DMA((3, 4)),
        ],
        compiler_params=pltpu.CompilerParams(vmem_limit_bytes=60 << 20),
    )(*results)


def solution(mesh):
    in_specs = (
        P("dp", "label"),
        P("dp", None),
        P("dp"),
        P(("dp", "label"), None),
        P(("dp", "label"), None),
        P(("dp", "label"), None),
    )
    out_specs = (P(("dp", "label"), None), P(("dp", "label"), None), P(("dp", "label"), None))
    return jax.shard_map(shards, mesh=mesh, in_specs=in_specs, out_specs=out_specs, check_vma=False)
```

```python
import jax
import jax.numpy as jnp
from jax import lax
from jax.experimental import pallas as pl
from jax.experimental.pallas import tpu as pltpu
from jax.sharding import PartitionSpec as P

STEP = 10
MESH = pl.DeviceIdType.MESH
NX, NY, NZ = 4, 4, 16
WIDTH, ROWS, QUERIES = 768, 256, 4096
HALF = WIDTH // 2
BLOCK_D, BLOCK_Q = 48, 128
SCALE = 1.0 / WIDTH**0.5
LOG2_E = 1.4426950408889634
N_SEMS = 230

GROUPS = {
    "own": (0, 1, "y"),
    "4": (4, 5, "x"),
    "12": (12, 13, "y"),
    "5": (5, 6, "x"),
    "11": (11, 12, "y"),
    "6": (6, 7, "x"),
    "10": (10, 11, "y"),
    "78": (7, 9, "x"),
    "9": (9, 10, "y"),
}
FORWARDED = ()
LAST = ()
OTHERS = (1, 3, 2)
NEAR_Z = (4, 12, 3, 13, 2, 14, 1, 15)
FAR_Z = (8, 7, 9, 6, 10, 5, 11)
PLANE = sorted(
    ((i, j, k) for i in range(NX) for j in range(NY) for k in range(2) if i or j or k),
    key=lambda o: -(min(o[0], NX - o[0]) + min(o[1], NY - o[1]) + o[2]),
)

ORDER = (
    ("h1", "own"), ("h2", "own"), ("lab", 0), ("zh", 4), ("zh", 12), ("h1", "4"), ("h1", "12"),
    ("fz", 0, 0), ("lab", 1), ("h1", "11"), ("h1", "5"), ("h2", "12"), ("h3", "own"), ("h1", "9"),
    ("h1", "6"), ("h2", "4"), ("h1", "10"), ("h1", "78"), ("fz", 1, 0), ("h2", "11"), ("greet",), ("lab", 2),
    ("h2", "9"), ("h2", "6"), ("fz", 0, 1), ("fz", 0, 2), ("fz", 0, 3), ("lab", 3), ("h2", "78"),
    ("fz", 2, 0), ("h2", "10"), ("h3", "4"), ("h3", "12"), ("h3", "6"), ("fz", 1, 1), ("p", 4),
    ("fz", 1, 2), ("fz", 1, 3), ("h2", "5"), ("h3", "11"), ("h3", "9"), ("h3", "10"), ("p", 6),
    ("h3", "78"), ("fz", 2, 1), ("p", 1, 2), ("fz", 2, 2), ("fz", 2, 3), ("h3", "5"),
    ("p", 0, 7, 3), ("p", 5),
)


def kernel(
    features, ids, count, weight, moment, second,
    update_hbm, moment_hbm, second_hbm, trust_hbm,
    feat_in, ids_in, count_in, ids_t, w_in, mom_in, sec_in, w_bf, held, labels, words, acc, sums,
    update_out, moment_out, second_out, trust_out, send, recv, local,
):
    dp, lb = lax.axis_index("dp"), lax.axis_index("label")
    x, y, core = lax.rem(lb // 2, NX), lax.rem(dp, NY), lax.rem(lb, 2)
    z = (lb // 8) * 8 + dp // NY

    def device(x, y, z, core):
        return {"dp": lax.rem(z, 8) * NY + y, "label": (z // 8) * 8 + x * 2 + core}

    def along(axis, by):
        if axis == "x":
            return device(lax.rem(x + by, NX), y, z, core)
        if axis == "y":
            return device(x, lax.rem(y + by, NY), z, core)
        if axis == "z":
            return device(x, y, lax.rem(z + by, NZ), core)
        return device(x, y, z, 1 - core)

    def in_plane(offset):
        i, j, k = offset
        return device(lax.rem(x + i, NX), lax.rem(y + j, NY), z, lax.rem(core + k, 2))

    loads = {}
    for i, (name, src, dst) in enumerate(
        [
            ("features", features, feat_in),
            ("ids", ids, ids_in),
            ("count", count, count_in),
            ("weight", weight, w_in),
            ("moment", moment, mom_in),
            ("second", second, sec_in),
        ]
    ):
        loads[name] = pltpu.make_async_copy(src, dst, local.at[i])
        loads[name].start()

    barrier = pltpu.get_barrier_semaphore()
    def greet(devices):
        for to in devices:
            pl.semaphore_signal(barrier, inc=1, device_id=to, device_id_type=MESH)

    near = [along("z", by) for by in NEAR_Z]
    near += [in_plane(o) for o in PLANE if sum(1 for i in o if i) == 1]
    greet(near)
    later = [along("z", by) for by in FAR_Z]
    later += [in_plane(o) for o in PLANE if sum(1 for i in o if i) > 1]

    loads["features"].wait()
    held[0, y, x, core] = feat_in[...]
    loads["ids"].wait()
    loads["count"].wait()
    used = lax.broadcasted_iota(jnp.int32, ids_in.shape, 0) < count_in[...]
    ids_t[...] = jnp.where(used, ids_in[...], -1).reshape(4, 8, BLOCK_Q)
    row, col = jnp.where(core == 0, y, x), jnp.where(core == 0, x, y)
    labels[3 + 5 * core, row, col] = ids_t[x]

    used_sems, sent = [0], []

    def sems():
        used_sems[0] += 1
        return send.at[used_sems[0] - 1], recv.at[used_sems[0] - 1]

    def copy(src, dst, to, recv_sem=None):
        s, r = sems()
        c = pltpu.make_async_remote_copy(
            src, dst, s, r if recv_sem is None else recv_sem, device_id=to, device_id_type=MESH
        )
        sent.append(c)
        c.start()
        return c

    def arrived(part, sem):
        pltpu.make_async_remote_copy(
            part, part, send.at[0], sem, device_id=along("z", 1), device_id_type=MESH
        ).wait_recv()

    pl.semaphore_wait(barrier, len(near))

    toward = 1 - 2 * core
    label_z = sems()[1]
    for k in (3, 2, 1, 0):
        to = device(x, y, lax.rem(z + toward * (k + 1) + NZ, NZ), core)
        there = 8 - core if k == 3 else (2 - k) * (1 - core) + (4 + k) * core
        copy(ids_t.at[x], labels.at[there, row, col], to, label_z)

    def label_hop(first, i):
        on_x = (core == 0) == first
        return device(
            jnp.where(on_x, lax.rem(x + i, NX), x), jnp.where(on_x, y, lax.rem(y + i, NY)), z, core
        )

    z_recv = {name: sems()[1] for name in GROUPS if name != "own"}

    def slot(r):
        found = [n for n, (a, b, _) in GROUPS.items() if a <= r < b]
        return found[0] if found else "z" + str(min(r, NZ - r))

    def block(r):
        return held.at[r, y, x, core]

    for r in (4, 12):
        copy(block(0), block(r), along("z", NZ - r), z_recv[slot(r)])

    def hand_on(first):
        arrived(block(first), z_recv[slot(first)])
        there = (8, 7, 6, 5) if first == 4 else (9, 10, 11)
        for r in there:
            by = (NZ + first - r) % NZ
            copy(block(first), block(r), along("z", by), z_recv[slot(r)])

    hops, cross = {}, {}

    def hop1(name):
        a, b, axis = GROUPS[name]
        part = held.at[a:b, y, x, core]
        if name not in ("own", "4", "12"):
            arrived(part, z_recv[name])
        hops[name] = [copy(part, part, along(axis, i)) for i in OTHERS]

    def line(name, at, part=slice(0, 4)):
        a, b, axis = GROUPS[name]
        return held.at[a:b, at, part, core] if axis == "x" else held.at[a:b, part, at, core]

    def to_core(name, part):
        cross.setdefault(name, []).append(copy(part, part, along("core", 1)))

    passed = [[], [], []]

    def to_z(k, at):
        ups = held.at[(NZ - k) % NZ, :, at, core], held.at[NZ - 1 - k, :, at, core]
        downs = held.at[k, :, at, core], held.at[k + 1, :, at, core]
        passed[k].append((copy(*ups, along("z", 1)), copy(*downs, along("z", NZ - 1))))

    def from_z(k, n):
        at = lax.rem(x + 4 - (0, *OTHERS)[n], 4)
        for c in passed[k][n]:
            c.wait_recv()
        if k < 2:
            to_z(k + 1, at)
        for r in (k + 1, NZ - 1 - k):
            if k == 2:
                to_core("z3", held.at[r, :, at, core])
            elif n == 3:
                to_core("z" + str(k + 1), held.at[r, :, :, core])

    def hop2(name):
        other, mine = ("y", y) if GROUPS[name][2] == "x" else ("x", x)
        for c in hops[name]:
            c.wait_recv()
        part = line(name, mine)
        to = OTHERS[:2] if name in FORWARDED else OTHERS
        hops[name] = [copy(part, part, along(other, i)) for i in to]
        if name == "own":
            to_z(0, mine)
        if name in LAST:
            to_core(name, part)

    def forward(name):
        other, mine = ("y", y) if GROUPS[name][2] == "x" else ("x", x)
        halves = []
        for c, i in zip(hops[name], OTHERS[:2], strict=True):
            c.wait_recv()
            at = lax.rem(mine + 4 - i, 4)
            part = line(name, at, slice(0, 2) if i == 1 else slice(2, 4))
            halves.append(copy(part, part, along(other, i)))
            if name in LAST:
                to_core(name, line(name, at))
        hops[name] = halves

    def hop3(name):
        a, b, axis = GROUPS[name]
        mine = y if axis == "x" else x
        for c, i in zip(hops[name], OTHERS, strict=False):
            c.wait_recv()
            at = lax.rem(mine + 4 - i, 4)
            if name == "own":
                to_z(0, at)
            if name in LAST and name not in FORWARDED:
                to_core(name, line(name, at))
        if name not in LAST:
            for r in range(a, b):
                to_core(name, held.at[r, :, :, core])
        elif name in FORWARDED:
            to_core(name, line(name, lax.rem(mine + 2, 4)))

    waiting = set()

    def done(name):
        if name not in waiting:
            waiting.add(name)
            for c in cross[name]:
                c.wait_recv()

    first = (dp * 16 + lb) * ROWS

    def mark(i, core):
        pos, at = i // NY, lax.rem(i, NY)
        if core == 0:
            pair, found = lax.rem(pos + 5, 8), labels[pos, at]
        else:
            pair, found = pos + 1, labels[4 + pos, :, at]
        local_id = found - first
        word = local_id >> 5
        bit = jnp.left_shift(jnp.int32(1), local_id & 31)
        rows = lax.broadcasted_iota(jnp.int32, (8, BLOCK_Q), 0)
        out = jnp.zeros((8, BLOCK_Q), jnp.int32)
        for w in range(8):
            hit = jnp.where(word == w, bit, 0)
            hit = (hit[0] | hit[1]) | (hit[2] | hit[3])
            for by in (4, 2, 1):
                hit = hit | pltpu.roll(hit, by, 0)
            out = jnp.where(rows == w, hit, out)
        words[pair, at] = out
        return core

    label_sent = []

    def label(stage):
        if stage == 0:
            arrived(labels.at[0:4, row, col], label_z)
        for c in label_sent:
            c.wait_recv()
        label_sent.clear()
        if stage == 0:
            part = labels.at[pl.ds(4 * core, 4), row, col]
            label_sent.extend(copy(part, part, label_hop(True, i)) for i in OTHERS)
        elif stage == 1:
            part = labels.at[pl.ds(4 * core, 4), row]
            label_sent.extend(copy(part, part, label_hop(False, i)) for i in OTHERS)
        elif stage == 2:
            part = labels.at[pl.ds(4 * core, 4)]
            label_sent.append(copy(part, part, along("core", 1)))
        else:
            for i in range(2):
                lax.fori_loop(0, 4 * NY, lambda n, _, i=i: (mark(n, i), 0)[1], 0)

    def pair(r):
        lo = lax.rem(z + r, NZ) // 8
        q = NY * BLOCK_Q

        def slab(at):
            return jnp.concatenate([held[at, i].reshape(HALF, BLOCK_Q) for i in range(NY)], axis=1)

        rows = jnp.concatenate([slab(r), slab(r + 8)], axis=0)
        both = jnp.concatenate([w_bf[lo], w_bf[1 - lo]], axis=1)
        scores = jnp.dot(both, rows, preferred_element_type=jnp.float32)
        prob = 1.0 / (1.0 + jnp.exp2(scores * (-SCALE * LOG2_E)))
        marks = jnp.concatenate([words[r, i] for i in range(NY)], axis=1)
        bits = jnp.left_shift(jnp.int32(1), lax.broadcasted_iota(jnp.int32, (32, q), 0))
        target = jnp.concatenate(
            [(jnp.broadcast_to(marks[w : w + 1], (32, q)) & bits) != 0 for w in range(8)], axis=0
        )
        dscore = (prob - jnp.where(target, 1.0, 0.0)).astype(jnp.bfloat16)
        dims = (((1,), (1,)), ((), ()))
        g = lax.dot_general(dscore, rows, dims, preferred_element_type=jnp.float32)
        acc[lo] += g[:, :HALF]
        acc[1 - lo] += g[:, HALF:]

    steps = {"zh": hand_on, "h1": hop1, "h2": hop2, "h2b": forward, "h3": hop3, "fz": from_z, "lab": label}
    for at, (what, *args) in enumerate(ORDER):
        if at == 2:
            loads["weight"].wait()
            w_bf[0] = w_in[:, :HALF].astype(jnp.bfloat16)
            w_bf[1] = w_in[:, HALF:].astype(jnp.bfloat16)
            acc[...] = jnp.zeros_like(acc)
        if what == "greet":
            done("own")
            greet(later)
            continue
        if what != "p":
            steps[what](*args)
            continue
        for r in args:
            done(slot(r))
            done(slot(r + 8))
        for r in args:
            pair(r)

    loads["moment"].wait()
    loads["second"].wait()
    step_rows = 32

    def refresh(i, carry):
        at = pl.ds(pl.multiple_of(i * step_rows, step_rows), step_rows)
        totals = list(carry)
        for h in range(2):
            cols = slice(h * HALF, (h + 1) * HALF)
            g = acc[h, at] * (SCALE / QUERIES)
            w = w_in[at, cols]
            m = 0.9 * mom_in[at, cols] + 0.1 * g
            v = 0.999 * sec_in[at, cols] + 0.001 * g * g
            u = (m * (1.0 / (1.0 - 0.9**STEP))) / (
                jnp.sqrt(v * (1.0 / (1.0 - 0.999**STEP))) + 1e-06
            ) + 0.01 * w
            update_out[at, cols] = u
            moment_out[at, cols] = m
            second_out[at, cols] = v
            for k, s in enumerate((w * w, u * u)):
                s = jnp.sum(s.reshape(step_rows // 8, 8, HALF), axis=0)
                totals[k] += s[:, :128] + s[:, 128:256] + s[:, 256:]
        return tuple(totals)

    zero = jnp.zeros((8, 128), jnp.float32)
    totals = lax.fori_loop(0, ROWS // step_rows, refresh, (zero, zero))
    stores = [
        pltpu.make_async_copy(update_out, update_hbm, local.at[6]),
        pltpu.make_async_copy(moment_out, moment_hbm, local.at[7]),
        pltpu.make_async_copy(second_out, second_hbm, local.at[8]),
    ]
    for c in stores:
        c.start()
    value = jnp.concatenate([jnp.sum(t, axis=0, keepdims=True) for t in totals], axis=0)

    pl.semaphore_wait(barrier, len(later))
    gathered = list(sent)
    base = 2
    column = [along("z", by) for by in (*FAR_Z, *NEAR_Z)]
    for stage, to in enumerate(([in_plane(o) for o in PLANE], column)):
        sums[stage] = value
        cs = [copy(sums.at[stage], sums.at[base + i], d) for i, d in enumerate(to)]
        for c in gathered[stage::2]:
            c.wait_send()
        for c in stores if stage else ():
            c.wait()
        for c in cs:
            c.wait_recv()
        value = value + jnp.sum(sums[base : base + len(to)], axis=0)
        base += len(to)
    norms = jnp.sqrt(jnp.sum(value, axis=1, keepdims=True))
    trust = norms[0:1] / (norms[1:2] + 1e-06)
    trust_out[...] = jnp.broadcast_to(trust, trust_out.shape)
    store = pltpu.make_async_copy(trust_out, trust_hbm, local.at[0])
    store.start()
    for c in sent[len(gathered) :]:
        c.wait_send()
    store.wait()


def finish(update, moment, second, trust, step_out, moment_out, second_out, held, scaled, by, given, done):
    parts, n = 4, ROWS // 4
    factor = pltpu.make_async_copy(trust, by, given.at[3, 0])
    factor.start()
    reads, writes = {}, []
    for i in range(parts):
        at = pl.ds(i * n, n)
        for k, src in enumerate((update, moment, second)):
            reads[k, i] = pltpu.make_async_copy(src.at[at], held.at[k, at], given.at[k, i])
            reads[k, i].start()
    factor.wait()
    for i in range(parts):
        at = pl.ds(i * n, n)
        for k, dst in enumerate((step_out, moment_out, second_out)):
            reads[k, i].wait()
            if k == 0:
                scaled[at] = held[0, at] * by[0:1, 0:1]
            src = scaled.at[at] if k == 0 else held.at[k, at]
            writes.append(pltpu.make_async_copy(src, dst.at[at], done.at[k, i]))
            writes[-1].start()
    for c in writes:
        c.wait()


def shards(features, label_ids, label_count, weight, moment, second):
    hbm = pl.BlockSpec(memory_space=pltpu.HBM)
    f32, bf16, i32 = jnp.float32, jnp.bfloat16, jnp.int32
    block = jax.ShapeDtypeStruct(weight.shape, f32)
    results = pl.pallas_call(
        kernel,
        name="step",
        out_shape=(block, block, block, jax.ShapeDtypeStruct((8, 128), f32)),
        in_specs=[hbm] * 6,
        out_specs=(hbm, hbm, hbm, hbm),
        scratch_shapes=[
            pltpu.VMEM(features.shape[::-1], bf16),
            pltpu.VMEM(label_ids.shape[::-1], i32),
            pltpu.VMEM((1, BLOCK_Q), i32),
            pltpu.VMEM((4, 8, BLOCK_Q), i32),
            pltpu.VMEM(weight.shape, f32),
            pltpu.VMEM(weight.shape, f32),
            pltpu.VMEM(weight.shape, f32),
            pltpu.VMEM((2, ROWS, HALF), bf16),
            pltpu.VMEM((NZ, NY, NX, 2, BLOCK_D, BLOCK_Q), bf16),
            pltpu.VMEM((9, NY, NX, 8, BLOCK_Q), i32),
            pltpu.VMEM((8, NY, 8, BLOCK_Q), i32),
            pltpu.VMEM((2, ROWS, HALF), f32),
            pltpu.VMEM((48, 2, 128), f32),
            pltpu.VMEM(weight.shape, f32),
            pltpu.VMEM(weight.shape, f32),
            pltpu.VMEM(weight.shape, f32),
            pltpu.VMEM((8, 128), f32),
            pltpu.SemaphoreType.DMA((N_SEMS,)),
            pltpu.SemaphoreType.DMA((N_SEMS,)),
            pltpu.SemaphoreType.DMA((9,)),
        ],
        compiler_params=pltpu.CompilerParams(
            collective_id=0, has_side_effects=True, vmem_limit_bytes=60 << 20
        ),
    )(features.T, label_ids.T, label_count.reshape(1, -1), weight, moment, second)
    return pl.pallas_call(
        finish,
        name="finish",
        out_shape=(block, block, block),
        in_specs=[hbm] * 4,
        out_specs=(hbm, hbm, hbm),
        scratch_shapes=[
            pltpu.VMEM((3, *weight.shape), f32),
            pltpu.VMEM(weight.shape, f32),
            pltpu.VMEM((8, 128), f32),
            pltpu.SemaphoreType.DMA((4, 4)),
            pltpu.SemaphoreType.DMA((3, 4)),
        ],
        compiler_params=pltpu.CompilerParams(vmem_limit_bytes=60 << 20),
    )(*results)


def solution(mesh):
    in_specs = (
        P("dp", "label"),
        P("dp", None),
        P("dp"),
        P(("dp", "label"), None),
        P(("dp", "label"), None),
        P(("dp", "label"), None),
    )
    out_specs = (P(("dp", "label"), None), P(("dp", "label"), None), P(("dp", "label"), None))
    return jax.shard_map(shards, mesh=mesh, in_specs=in_specs, out_specs=out_specs, check_vma=False)
```

```python
import jax
import jax.numpy as jnp
from jax import lax
from jax.experimental import pallas as pl
from jax.experimental.pallas import tpu as pltpu
from jax.sharding import PartitionSpec as P

STEP = 10
MESH = pl.DeviceIdType.MESH
NX, NY, NZ = 4, 4, 16
WIDTH, ROWS, QUERIES = 768, 256, 4096
HALF = WIDTH // 2
BLOCK_D, BLOCK_Q = 48, 128
SCALE = 1.0 / WIDTH**0.5
LOG2_E = 1.4426950408889634
KINDS = ("label", "z", "hop1", "hop2", "up_down", "core", "plane", "column")
N_ARRIVALS = 58

GROUPS = {
    "own": (0, 1, "y"),
    "4": (4, 5, "x"),
    "12": (12, 13, "y"),
    "5": (5, 6, "x"),
    "11": (11, 12, "y"),
    "6": (6, 7, "x"),
    "10": (10, 11, "y"),
    "78": (7, 9, "x"),
    "9": (9, 10, "y"),
}
OTHERS = (1, 3, 2)
NEAR_Z = (4, 12, 3, 13, 2, 14, 1, 15)
FAR_Z = (8, 7, 9, 6, 10, 5, 11)
PLANE = sorted(
    ((i, j, k) for i in range(NX) for j in range(NY) for k in range(2) if i or j or k),
    key=lambda o: -(min(o[0], NX - o[0]) + min(o[1], NY - o[1]) + o[2]),
)

ORDER = (
    ("h1", "own"), ("h2", "own"), ("lab", 0), ("zh", 4), ("zh", 12), ("h1", "4"), ("h1", "12"),
    ("fz", 0, 0), ("lab", 1), ("h1", "11"), ("h1", "5"), ("h2", "12"), ("h3", "own"), ("h1", "9"),
    ("h1", "6"), ("h2", "4"), ("h1", "10"), ("h1", "78"), ("fz", 1, 0), ("h2", "11"), ("greet",), ("lab", 2),
    ("h2", "9"), ("h2", "6"), ("fz", 0, 1), ("fz", 0, 2), ("fz", 0, 3), ("lab", 3), ("h2", "78"),
    ("fz", 2, 0), ("h2", "10"), ("h3", "4"), ("h3", "12"), ("h3", "6"), ("fz", 1, 1), ("p", 4),
    ("fz", 1, 2), ("fz", 1, 3), ("h2", "5"), ("h3", "11"), ("h3", "9"), ("h3", "10"), ("p", 6),
    ("h3", "78"), ("fz", 2, 1), ("p", 1, 2), ("fz", 2, 2), ("fz", 2, 3), ("h3", "5"),
    ("p", 0, 7, 3), ("p", 5),
)


def kernel(
    features, ids, count, weight, moment, second,
    update_hbm, moment_hbm, second_hbm, trust_hbm,
    feat_in, ids_in, count_in, ids_t, w_in, mom_in, sec_in, w_bf, held, labels, words, acc, sums,
    update_out, moment_out, second_out, trust_out, send, recv, local,
):
    dp, lb = lax.axis_index("dp"), lax.axis_index("label")
    x, y, core = lax.rem(lb // 2, NX), lax.rem(dp, NY), lax.rem(lb, 2)
    z = (lb // 8) * 8 + dp // NY

    def device(x, y, z, core):
        return {"dp": lax.rem(z, 8) * NY + y, "label": (z // 8) * 8 + x * 2 + core}

    def along(axis, by):
        if axis == "x":
            return device(lax.rem(x + by, NX), y, z, core)
        if axis == "y":
            return device(x, lax.rem(y + by, NY), z, core)
        if axis == "z":
            return device(x, y, lax.rem(z + by, NZ), core)
        return device(x, y, z, 1 - core)

    def in_plane(offset):
        i, j, k = offset
        return device(lax.rem(x + i, NX), lax.rem(y + j, NY), z, lax.rem(core + k, 2))

    loads = {}
    for i, (name, src, dst) in enumerate(
        [
            ("features", features, feat_in),
            ("ids", ids, ids_in),
            ("count", count, count_in),
            ("weight", weight, w_in),
            ("moment", moment, mom_in),
            ("second", second, sec_in),
        ]
    ):
        loads[name] = pltpu.make_async_copy(src, dst, local.at[i])
        loads[name].start()

    barrier = pltpu.get_barrier_semaphore()
    def greet(devices):
        for to in devices:
            pl.semaphore_signal(barrier, inc=1, device_id=to, device_id_type=MESH)

    near = [along("z", by) for by in NEAR_Z]
    near += [in_plane(o) for o in PLANE if sum(1 for i in o if i) == 1]
    greet(near)
    later = [along("z", by) for by in FAR_Z]
    later += [in_plane(o) for o in PLANE if sum(1 for i in o if i) > 1]

    loads["features"].wait()
    held[0, y, x, core] = feat_in[...]
    loads["ids"].wait()
    loads["count"].wait()
    used = lax.broadcasted_iota(jnp.int32, ids_in.shape, 0) < count_in[...]
    ids_t[...] = jnp.where(used, ids_in[...], -1).reshape(4, 8, BLOCK_Q)
    row, col = jnp.where(core == 0, y, x), jnp.where(core == 0, x, y)
    labels[3 + 5 * core, row, col] = ids_t[x]

    arrivals = {}

    def arrival(key):
        return recv.at[arrivals.setdefault(key, len(arrivals))]

    def described(src, dst, to, kind, key):
        return pltpu.make_async_remote_copy(
            src, dst, send.at[KINDS.index(kind)], arrival(key), device_id=to, device_id_type=MESH
        )

    def copy(src, dst, to, kind, key):
        described(src, dst, to, kind, key).start()

    def arrived(part, key):
        described(part, part, along("z", 1), "z", key).wait_recv()

    def blocks(n):
        if n <= NZ:
            return held.at[0:n, 0, 0, 0]
        return held.at[0 : n // 4, :, 0, 0] if n < 64 else held.at[0 : n // 32]

    pl.semaphore_wait(barrier, len(near))

    toward = 1 - 2 * core
    for k in (3, 2, 1, 0):
        to = device(x, y, lax.rem(z + toward * (k + 1) + NZ, NZ), core)
        there = 8 - core if k == 3 else (2 - k) * (1 - core) + (4 + k) * core
        copy(ids_t.at[x], labels.at[there, row, col], to, "label", ("label", 0))

    def label_hop(first, i):
        on_x = (core == 0) == first
        return device(
            jnp.where(on_x, lax.rem(x + i, NX), x), jnp.where(on_x, y, lax.rem(y + i, NY)), z, core
        )

    def slot(r):
        found = [n for n, (a, b, _) in GROUPS.items() if a <= r < b]
        return found[0] if found else "z" + str(min(r, NZ - r))

    def block(r):
        return held.at[r, y, x, core]

    for r in (4, 12):
        copy(block(0), block(r), along("z", NZ - r), "z", ("z", slot(r)))

    def hand_on(first):
        arrived(block(first), ("z", slot(first)))
        there = (8, 7, 6, 5) if first == 4 else (9, 10, 11)
        for r in there:
            by = (NZ + first - r) % NZ
            copy(block(first), block(r), along("z", by), "z", ("z", slot(r)))

    crossing = {}

    def hop1(name):
        a, b, axis = GROUPS[name]
        part = held.at[a:b, y, x, core]
        if name not in ("own", "4", "12"):
            arrived(part, ("z", name))
        for i in OTHERS:
            copy(part, part, along(axis, i), "hop1", ("hop1", name))

    def to_core(name, part, n):
        crossing[name] = crossing.get(name, 0) + n
        copy(part, part, along("core", 1), "core", ("core", name))

    def to_z(k, n, at):
        ups = held.at[(NZ - k) % NZ, :, at, core], held.at[NZ - 1 - k, :, at, core]
        downs = held.at[k, :, at, core], held.at[k + 1, :, at, core]
        copy(*ups, along("z", 1), "up_down", ("up_down", k, n))
        copy(*downs, along("z", NZ - 1), "up_down", ("up_down", k, n))

    def from_z(k, n):
        at = lax.rem(x + 4 - (0, *OTHERS)[n], 4)
        arrived(blocks(8), ("up_down", k, n))
        if k < 2:
            to_z(k + 1, n, at)
        for r in (k + 1, NZ - 1 - k):
            if k == 2:
                to_core("z3", held.at[r, :, at, core], 4)
            elif n == 3:
                to_core("z" + str(k + 1), held.at[r, :, :, core], 16)

    def hop2(name):
        a, b, axis = GROUPS[name]
        arrived(blocks(3 * (b - a)), ("hop1", name))
        part = held.at[a:b, y, :, core] if axis == "x" else held.at[a:b, :, x, core]
        for n, i in enumerate(OTHERS):
            key = ("hop2", name, n) if name == "own" else ("hop2", name)
            copy(part, part, along("y" if axis == "x" else "x", i), "hop2", key)
        if name == "own":
            to_z(0, 0, x)

    def hop3(name):
        a, b, _ = GROUPS[name]
        if name == "own":
            for n, i in enumerate(OTHERS):
                arrived(blocks(4), ("hop2", name, n))
                to_z(0, n + 1, lax.rem(x + 4 - i, 4))
        else:
            arrived(blocks(12 * (b - a)), ("hop2", name))
        for r in range(a, b):
            to_core(name, held.at[r, :, :, core], 16)

    waiting = set()

    def done(name):
        if name not in waiting:
            waiting.add(name)
            arrived(blocks(crossing[name]), ("core", name))

    first = (dp * 16 + lb) * ROWS

    def mark(i, core):
        pos, at = i // NY, lax.rem(i, NY)
        if core == 0:
            pair, found = lax.rem(pos + 5, 8), labels[pos, at]
        else:
            pair, found = pos + 1, labels[4 + pos, :, at]
        local_id = found - first
        word = local_id >> 5
        bit = jnp.left_shift(jnp.int32(1), local_id & 31)
        rows = lax.broadcasted_iota(jnp.int32, (8, BLOCK_Q), 0)
        out = jnp.zeros((8, BLOCK_Q), jnp.int32)
        for w in range(8):
            hit = jnp.where(word == w, bit, 0)
            hit = (hit[0] | hit[1]) | (hit[2] | hit[3])
            for by in (4, 2, 1):
                hit = hit | pltpu.roll(hit, by, 0)
            out = jnp.where(rows == w, hit, out)
        words[pair, at] = out
        return core

    def label(stage):
        part = labels.at[0 : (0, 0, 3, 4)[stage]] if stage > 1 else labels.at[0 : 4 - stage, 0]
        arrived(part if stage else labels.at[0:4, 0, 0], ("label", stage))
        if stage == 3:
            for i in range(2):
                lax.fori_loop(0, 4 * NY, lambda n, _, i=i: (mark(n, i), 0)[1], 0)
            return
        mine = labels.at[pl.ds(4 * core, 4)]
        part = (mine.at[:, row, col], mine.at[:, row], mine)[stage]
        to = [label_hop(stage == 0, i) for i in OTHERS] if stage < 2 else [along("core", 1)]
        for d in to:
            copy(part, part, d, "label", ("label", stage + 1))

    def pair(r):
        lo = lax.rem(z + r, NZ) // 8
        q = NY * BLOCK_Q

        def slab(at):
            return jnp.concatenate([held[at, i].reshape(HALF, BLOCK_Q) for i in range(NY)], axis=1)

        rows = jnp.concatenate([slab(r), slab(r + 8)], axis=0)
        both = jnp.concatenate([w_bf[lo], w_bf[1 - lo]], axis=1)
        scores = jnp.dot(both, rows, preferred_element_type=jnp.float32)
        prob = 1.0 / (1.0 + jnp.exp2(scores * (-SCALE * LOG2_E)))
        marks = jnp.concatenate([words[r, i] for i in range(NY)], axis=1)
        bits = jnp.left_shift(jnp.int32(1), lax.broadcasted_iota(jnp.int32, (32, q), 0))
        target = jnp.concatenate(
            [(jnp.broadcast_to(marks[w : w + 1], (32, q)) & bits) != 0 for w in range(8)], axis=0
        )
        dscore = (prob - jnp.where(target, 1.0, 0.0)).astype(jnp.bfloat16)
        dims = (((1,), (1,)), ((), ()))
        g = lax.dot_general(dscore, rows, dims, preferred_element_type=jnp.float32)
        acc[lo] += g[:, :HALF]
        acc[1 - lo] += g[:, HALF:]

    steps = {"zh": hand_on, "h1": hop1, "h2": hop2, "h3": hop3, "fz": from_z, "lab": label}
    for at, (what, *args) in enumerate(ORDER):
        if at == 2:
            loads["weight"].wait()
            w_bf[0] = w_in[:, :HALF].astype(jnp.bfloat16)
            w_bf[1] = w_in[:, HALF:].astype(jnp.bfloat16)
            acc[...] = jnp.zeros_like(acc)
        if what == "greet":
            done("own")
            greet(later)
            continue
        if what != "p":
            steps[what](*args)
            continue
        for r in args:
            done(slot(r))
            done(slot(r + 8))
        for r in args:
            pair(r)

    loads["moment"].wait()
    loads["second"].wait()
    step_rows = 32

    def refresh(i, carry):
        at = pl.ds(pl.multiple_of(i * step_rows, step_rows), step_rows)
        totals = list(carry)
        for h in range(2):
            cols = slice(h * HALF, (h + 1) * HALF)
            g = acc[h, at] * (SCALE / QUERIES)
            w = w_in[at, cols]
            m = 0.9 * mom_in[at, cols] + 0.1 * g
            v = 0.999 * sec_in[at, cols] + 0.001 * g * g
            u = (m * (1.0 / (1.0 - 0.9**STEP))) / (
                jnp.sqrt(v * (1.0 / (1.0 - 0.999**STEP))) + 1e-06
            ) + 0.01 * w
            update_out[at, cols] = u
            moment_out[at, cols] = m
            second_out[at, cols] = v
            for k, s in enumerate((w * w, u * u)):
                s = jnp.sum(s.reshape(step_rows // 8, 8, HALF), axis=0)
                totals[k] += s[:, :128] + s[:, 128:256] + s[:, 256:]
        return tuple(totals)

    zero = jnp.zeros((8, 128), jnp.float32)
    totals = lax.fori_loop(0, ROWS // step_rows, refresh, (zero, zero))
    stores = [
        pltpu.make_async_copy(update_out, update_hbm, local.at[6]),
        pltpu.make_async_copy(moment_out, moment_hbm, local.at[7]),
        pltpu.make_async_copy(second_out, second_hbm, local.at[8]),
    ]
    for c in stores:
        c.start()
    value = jnp.concatenate([jnp.sum(t, axis=0, keepdims=True) for t in totals], axis=0)

    pl.semaphore_wait(barrier, len(later))
    base = 2
    column = [along("z", by) for by in (*FAR_Z, *NEAR_Z)]
    left = {
        "label": labels.at[0:8],
        "z": held.at[0:9, 0, 0, 0],
        "hop1": held.at[0:15, 0:2, 0, 0],
        "hop2": held.at[0:15, :, 0:2, 0],
        "up_down": held.at[0:3],
        "core": held.at[0:8],
    }

    def have_left(kind, part):
        described(part, part, along("z", 1), kind, ("label", 0)).wait_send()

    for stage, to in enumerate(([in_plane(o) for o in PLANE], column)):
        kind = ("plane", "column")[stage]
        sums[stage] = value
        for i, d in enumerate(to):
            copy(sums.at[stage], sums.at[base + i], d, kind, kind)
        if stage:
            for c in stores:
                c.wait()
        else:
            for sent, part in left.items():
                have_left(sent, part)
        arrived(sums.at[base : base + len(to)], kind)
        value = value + jnp.sum(sums[base : base + len(to)], axis=0)
        base += len(to)
    norms = jnp.sqrt(jnp.sum(value, axis=1, keepdims=True))
    trust = norms[0:1] / (norms[1:2] + 1e-06)
    trust_out[...] = jnp.broadcast_to(trust, trust_out.shape)
    store = pltpu.make_async_copy(trust_out, trust_hbm, local.at[0])
    store.start()
    have_left("plane", sums.at[0 : len(PLANE)])
    have_left("column", sums.at[0 : len(column)])
    store.wait()


def finish(update, moment, second, trust, step_out, moment_out, second_out, held, scaled, by, given, done):
    parts, n = 4, ROWS // 4
    factor = pltpu.make_async_copy(trust, by, given.at[3, 0])
    factor.start()
    reads, writes = {}, []
    for i in range(parts):
        at = pl.ds(i * n, n)
        for k, src in enumerate((update, moment, second)):
            reads[k, i] = pltpu.make_async_copy(src.at[at], held.at[k, at], given.at[k, i])
            reads[k, i].start()
    factor.wait()
    for i in range(parts):
        at = pl.ds(i * n, n)
        for k, dst in enumerate((step_out, moment_out, second_out)):
            reads[k, i].wait()
            if k == 0:
                scaled[at] = held[0, at] * by[0:1, 0:1]
            src = scaled.at[at] if k == 0 else held.at[k, at]
            writes.append(pltpu.make_async_copy(src, dst.at[at], done.at[k, i]))
            writes[-1].start()
    for c in writes:
        c.wait()


def shards(features, label_ids, label_count, weight, moment, second):
    hbm = pl.BlockSpec(memory_space=pltpu.HBM)
    f32, bf16, i32 = jnp.float32, jnp.bfloat16, jnp.int32
    block = jax.ShapeDtypeStruct(weight.shape, f32)
    results = pl.pallas_call(
        kernel,
        name="step",
        out_shape=(block, block, block, jax.ShapeDtypeStruct((8, 128), f32)),
        in_specs=[hbm] * 6,
        out_specs=(hbm, hbm, hbm, hbm),
        scratch_shapes=[
            pltpu.VMEM(features.shape[::-1], bf16),
            pltpu.VMEM(label_ids.shape[::-1], i32),
            pltpu.VMEM((1, BLOCK_Q), i32),
            pltpu.VMEM((4, 8, BLOCK_Q), i32),
            pltpu.VMEM(weight.shape, f32),
            pltpu.VMEM(weight.shape, f32),
            pltpu.VMEM(weight.shape, f32),
            pltpu.VMEM((2, ROWS, HALF), bf16),
            pltpu.VMEM((NZ, NY, NX, 2, BLOCK_D, BLOCK_Q), bf16),
            pltpu.VMEM((9, NY, NX, 8, BLOCK_Q), i32),
            pltpu.VMEM((8, NY, 8, BLOCK_Q), i32),
            pltpu.VMEM((2, ROWS, HALF), f32),
            pltpu.VMEM((48, 2, 128), f32),
            pltpu.VMEM(weight.shape, f32),
            pltpu.VMEM(weight.shape, f32),
            pltpu.VMEM(weight.shape, f32),
            pltpu.VMEM((8, 128), f32),
            pltpu.SemaphoreType.DMA((len(KINDS),)),
            pltpu.SemaphoreType.DMA((N_ARRIVALS,)),
            pltpu.SemaphoreType.DMA((9,)),
        ],
        compiler_params=pltpu.CompilerParams(
            collective_id=0, has_side_effects=True, vmem_limit_bytes=60 << 20
        ),
    )(features.T, label_ids.T, label_count.reshape(1, -1), weight, moment, second)
    return pl.pallas_call(
        finish,
        name="finish",
        out_shape=(block, block, block),
        in_specs=[hbm] * 4,
        out_specs=(hbm, hbm, hbm),
        scratch_shapes=[
            pltpu.VMEM((3, *weight.shape), f32),
            pltpu.VMEM(weight.shape, f32),
            pltpu.VMEM((8, 128), f32),
            pltpu.SemaphoreType.DMA((4, 4)),
            pltpu.SemaphoreType.DMA((3, 4)),
        ],
        compiler_params=pltpu.CompilerParams(vmem_limit_bytes=60 << 20),
    )(*results)


def solution(mesh):
    in_specs = (
        P("dp", "label"),
        P("dp", None),
        P("dp"),
        P(("dp", "label"), None),
        P(("dp", "label"), None),
        P(("dp", "label"), None),
    )
    out_specs = (P(("dp", "label"), None), P(("dp", "label"), None), P(("dp", "label"), None))
    return jax.shard_map(shards, mesh=mesh, in_specs=in_specs, out_specs=out_specs, check_vma=False)
```

```python
import jax
import jax.numpy as jnp
from jax import lax
from jax.experimental import pallas as pl
from jax.experimental.pallas import tpu as pltpu
from jax.sharding import PartitionSpec as P

STEP = 10
MESH = pl.DeviceIdType.MESH
NX, NY, NZ = 4, 4, 16
WIDTH, ROWS, QUERIES = 768, 256, 4096
HALF = WIDTH // 2
BLOCK_D, BLOCK_Q = 48, 128
SCALE = 1.0 / WIDTH**0.5
LOG2_E = 1.4426950408889634
KINDS = ("label", "z", "hop1", "hop2", "up_down", "core", "plane", "column")
N_ARRIVALS = 58

GROUPS = {
    "own": (0, 1, "y"),
    "4": (4, 5, "x"),
    "12": (12, 13, "y"),
    "5": (5, 6, "x"),
    "11": (11, 12, "y"),
    "6": (6, 7, "x"),
    "10": (10, 11, "y"),
    "78": (7, 9, "x"),
    "9": (9, 10, "y"),
}
OTHERS = (1, 3, 2)
NEAR_Z = (4, 12, 3, 13, 2, 14, 1, 15)
FAR_Z = (8, 7, 9, 6, 10, 5, 11)
PLANE = sorted(
    ((i, j, k) for i in range(NX) for j in range(NY) for k in range(2) if i or j or k),
    key=lambda o: -(min(o[0], NX - o[0]) + min(o[1], NY - o[1]) + o[2]),
)

ORDER = (
    ("h1", "own"), ("h2", "own"), ("lab", 0), ("zh", 4), ("zh", 12), ("h1", "4"), ("h1", "12"),
    ("fz", 0, 0), ("lab", 1), ("h1", "11"), ("h1", "5"), ("h2", "12"), ("h3", "own"), ("h1", "9"),
    ("h1", "6"), ("h2", "4"), ("h1", "10"), ("h1", "78"), ("fz", 1, 0), ("h2", "11"), ("greet",), ("lab", 2),
    ("h2", "9"), ("h2", "6"), ("fz", 0, 1), ("fz", 0, 2), ("fz", 0, 3), ("lab", 3), ("h2", "78"),
    ("fz", 2, 0), ("h2", "10"), ("h3", "4"), ("h3", "12"), ("h3", "6"), ("fz", 1, 1), ("p", 4),
    ("fz", 1, 2), ("fz", 1, 3), ("h2", "5"), ("h3", "11"), ("h3", "9"), ("h3", "10"), ("p", 6),
    ("h3", "78"), ("fz", 2, 1), ("p", 1, 2), ("fz", 2, 2), ("fz", 2, 3), ("h3", "5"),
    ("p", 0, 7, 3), ("p", 5),
)


def kernel(
    packed, weight, moment, second,
    update_out, moment_out, second_out, trust_out,
    ids_t, w_in, mom_in, sec_in, w_bf, held, labels, words, acc, sums,
    send, recv, local,
):
    dp, lb = lax.axis_index("dp"), lax.axis_index("label")
    x, y, core = lax.rem(lb // 2, NX), lax.rem(dp, NY), lax.rem(lb, 2)
    z = (lb // 8) * 8 + dp // NY

    def device(x, y, z, core):
        return {"dp": lax.rem(z, 8) * NY + y, "label": (z // 8) * 8 + x * 2 + core}

    def along(axis, by):
        if axis == "x":
            return device(lax.rem(x + by, NX), y, z, core)
        if axis == "y":
            return device(x, lax.rem(y + by, NY), z, core)
        if axis == "z":
            return device(x, y, lax.rem(z + by, NZ), core)
        return device(x, y, z, 1 - core)

    def in_plane(offset):
        i, j, k = offset
        return device(lax.rem(x + i, NX), lax.rem(y + j, NY), z, lax.rem(core + k, 2))

    loads = {}
    for i, (name, src, dst) in enumerate(
        [
            ("weight", weight, w_in),
            ("moment", moment, mom_in),
            ("second", second, sec_in),
        ]
    ):
        loads[name] = pltpu.make_async_copy(src, dst, local.at[i])
        loads[name].start()

    barrier = pltpu.get_barrier_semaphore()
    def greet(devices):
        for to in devices:
            pl.semaphore_signal(barrier, inc=1, device_id=to, device_id_type=MESH)

    near = [along("z", by) for by in NEAR_Z]
    near += [in_plane(o) for o in PLANE if sum(1 for i in o if i) == 1]
    greet(near)
    later = [along("z", by) for by in FAR_Z]
    later += [in_plane(o) for o in PLANE if sum(1 for i in o if i) > 1]

    held[0, y, x, core] = packed[:BLOCK_D].astype(jnp.bfloat16)
    ids_t[...] = packed[BLOCK_D:].astype(jnp.int32).reshape(4, 8, BLOCK_Q)
    row, col = jnp.where(core == 0, y, x), jnp.where(core == 0, x, y)
    labels[3 + 5 * core, row, col] = ids_t[x]

    arrivals = {}

    def arrival(key):
        return recv.at[arrivals.setdefault(key, len(arrivals))]

    def described(src, dst, to, kind, key):
        return pltpu.make_async_remote_copy(
            src, dst, send.at[KINDS.index(kind)], arrival(key), device_id=to, device_id_type=MESH
        )

    def copy(src, dst, to, kind, key):
        described(src, dst, to, kind, key).start()

    def arrived(part, key):
        described(part, part, along("z", 1), "z", key).wait_recv()

    def blocks(n):
        if n <= NZ:
            return held.at[0:n, 0, 0, 0]
        return held.at[0 : n // 4, :, 0, 0] if n < 64 else held.at[0 : n // 32]

    pl.semaphore_wait(barrier, len(near))

    toward = 1 - 2 * core
    for k in (3, 2, 1, 0):
        to = device(x, y, lax.rem(z + toward * (k + 1) + NZ, NZ), core)
        there = 8 - core if k == 3 else (2 - k) * (1 - core) + (4 + k) * core
        copy(ids_t.at[x], labels.at[there, row, col], to, "label", ("label", 0))

    def label_hop(first, i):
        on_x = (core == 0) == first
        return device(
            jnp.where(on_x, lax.rem(x + i, NX), x), jnp.where(on_x, y, lax.rem(y + i, NY)), z, core
        )

    def slot(r):
        found = [n for n, (a, b, _) in GROUPS.items() if a <= r < b]
        return found[0] if found else "z" + str(min(r, NZ - r))

    def block(r):
        return held.at[r, y, x, core]

    for r in (4, 12):
        copy(block(0), block(r), along("z", NZ - r), "z", ("z", slot(r)))

    def hand_on(first):
        arrived(block(first), ("z", slot(first)))
        there = (8, 7, 6, 5) if first == 4 else (9, 10, 11)
        for r in there:
            by = (NZ + first - r) % NZ
            copy(block(first), block(r), along("z", by), "z", ("z", slot(r)))

    crossing = {}

    def hop1(name):
        a, b, axis = GROUPS[name]
        part = held.at[a:b, y, x, core]
        if name not in ("own", "4", "12"):
            arrived(part, ("z", name))
        for i in OTHERS:
            copy(part, part, along(axis, i), "hop1", ("hop1", name))

    def to_core(name, part, n):
        crossing[name] = crossing.get(name, 0) + n
        copy(part, part, along("core", 1), "core", ("core", name))

    def to_z(k, n, at):
        ups = held.at[(NZ - k) % NZ, :, at, core], held.at[NZ - 1 - k, :, at, core]
        downs = held.at[k, :, at, core], held.at[k + 1, :, at, core]
        copy(*ups, along("z", 1), "up_down", ("up_down", k, n))
        copy(*downs, along("z", NZ - 1), "up_down", ("up_down", k, n))

    def from_z(k, n):
        at = lax.rem(x + 4 - (0, *OTHERS)[n], 4)
        arrived(blocks(8), ("up_down", k, n))
        if k < 2:
            to_z(k + 1, n, at)
        for r in (k + 1, NZ - 1 - k):
            if k == 2:
                to_core("z3", held.at[r, :, at, core], 4)
            elif n == 3:
                to_core("z" + str(k + 1), held.at[r, :, :, core], 16)

    def hop2(name):
        a, b, axis = GROUPS[name]
        arrived(blocks(3 * (b - a)), ("hop1", name))
        part = held.at[a:b, y, :, core] if axis == "x" else held.at[a:b, :, x, core]
        for n, i in enumerate(OTHERS):
            key = ("hop2", name, n) if name == "own" else ("hop2", name)
            copy(part, part, along("y" if axis == "x" else "x", i), "hop2", key)
        if name == "own":
            to_z(0, 0, x)

    def hop3(name):
        a, b, _ = GROUPS[name]
        if name == "own":
            for n, i in enumerate(OTHERS):
                arrived(blocks(4), ("hop2", name, n))
                to_z(0, n + 1, lax.rem(x + 4 - i, 4))
        else:
            arrived(blocks(12 * (b - a)), ("hop2", name))
        for r in range(a, b):
            to_core(name, held.at[r, :, :, core], 16)

    waiting = set()

    def done(name):
        if name not in waiting:
            waiting.add(name)
            arrived(blocks(crossing[name]), ("core", name))

    first = (dp * 16 + lb) * ROWS

    def mark(i, core):
        pos, at = i // NY, lax.rem(i, NY)
        if core == 0:
            pair, found = lax.rem(pos + 5, 8), labels[pos, at]
        else:
            pair, found = pos + 1, labels[4 + pos, :, at]
        local_id = found - first
        word = local_id >> 5
        bit = jnp.left_shift(jnp.int32(1), local_id & 31)
        rows = lax.broadcasted_iota(jnp.int32, (8, BLOCK_Q), 0)
        out = jnp.zeros((8, BLOCK_Q), jnp.int32)
        for w in range(8):
            hit = jnp.where(word == w, bit, 0)
            hit = (hit[0] | hit[1]) | (hit[2] | hit[3])
            for by in (4, 2, 1):
                hit = hit | pltpu.roll(hit, by, 0)
            out = jnp.where(rows == w, hit, out)
        words[pair, at] = out
        return core

    def label(stage):
        part = labels.at[0 : (0, 0, 3, 4)[stage]] if stage > 1 else labels.at[0 : 4 - stage, 0]
        arrived(part if stage else labels.at[0:4, 0, 0], ("label", stage))
        if stage == 3:
            for i in range(2):
                lax.fori_loop(0, 4 * NY, lambda n, _, i=i: (mark(n, i), 0)[1], 0)
            return
        mine = labels.at[pl.ds(4 * core, 4)]
        part = (mine.at[:, row, col], mine.at[:, row], mine)[stage]
        to = [label_hop(stage == 0, i) for i in OTHERS] if stage < 2 else [along("core", 1)]
        for d in to:
            copy(part, part, d, "label", ("label", stage + 1))

    def pair(r):
        lo = lax.rem(z + r, NZ) // 8
        q = NY * BLOCK_Q

        def slab(at):
            return jnp.concatenate([held[at, i].reshape(HALF, BLOCK_Q) for i in range(NY)], axis=1)

        rows = jnp.concatenate([slab(r), slab(r + 8)], axis=0)
        both = jnp.concatenate([w_bf[lo], w_bf[1 - lo]], axis=1)
        scores = jnp.dot(both, rows, preferred_element_type=jnp.float32)
        prob = 1.0 / (1.0 + jnp.exp2(scores * (-SCALE * LOG2_E)))
        marks = jnp.concatenate([words[r, i] for i in range(NY)], axis=1)
        bits = jnp.left_shift(jnp.int32(1), lax.broadcasted_iota(jnp.int32, (32, q), 0))
        target = jnp.concatenate(
            [(jnp.broadcast_to(marks[w : w + 1], (32, q)) & bits) != 0 for w in range(8)], axis=0
        )
        dscore = (prob - jnp.where(target, 1.0, 0.0)).astype(jnp.bfloat16)
        dims = (((1,), (1,)), ((), ()))
        g = lax.dot_general(dscore, rows, dims, preferred_element_type=jnp.float32)
        acc[lo] += g[:, :HALF]
        acc[1 - lo] += g[:, HALF:]

    steps = {"zh": hand_on, "h1": hop1, "h2": hop2, "h3": hop3, "fz": from_z, "lab": label}
    for at, (what, *args) in enumerate(ORDER):
        if at == 2:
            loads["weight"].wait()
            w_bf[0] = w_in[:, :HALF].astype(jnp.bfloat16)
            w_bf[1] = w_in[:, HALF:].astype(jnp.bfloat16)
            acc[...] = jnp.zeros_like(acc)
        if what == "greet":
            done("own")
            greet(later)
            continue
        if what != "p":
            steps[what](*args)
            continue
        for r in args:
            done(slot(r))
            done(slot(r + 8))
        for r in args:
            pair(r)

    loads["moment"].wait()
    loads["second"].wait()
    step_rows = 32

    def refresh(i, carry):
        at = pl.ds(pl.multiple_of(i * step_rows, step_rows), step_rows)
        totals = list(carry)
        for h in range(2):
            cols = slice(h * HALF, (h + 1) * HALF)
            g = acc[h, at] * (SCALE / QUERIES)
            w = w_in[at, cols]
            m = 0.9 * mom_in[at, cols] + 0.1 * g
            v = 0.999 * sec_in[at, cols] + 0.001 * g * g
            u = (m * (1.0 / (1.0 - 0.9**STEP))) / (
                jnp.sqrt(v * (1.0 / (1.0 - 0.999**STEP))) + 1e-06
            ) + 0.01 * w
            update_out[at, cols] = u
            moment_out[at, cols] = m
            second_out[at, cols] = v
            for k, s in enumerate((w * w, u * u)):
                s = jnp.sum(s.reshape(step_rows // 8, 8, HALF), axis=0)
                totals[k] += s[:, :128] + s[:, 128:256] + s[:, 256:]
        return tuple(totals)

    zero = jnp.zeros((8, 128), jnp.float32)
    totals = lax.fori_loop(0, ROWS // step_rows, refresh, (zero, zero))
    value = jnp.concatenate([jnp.sum(t, axis=0, keepdims=True) for t in totals], axis=0)

    pl.semaphore_wait(barrier, len(later))
    base = 2
    column = [along("z", by) for by in (*FAR_Z, *NEAR_Z)]
    left = {
        "label": labels.at[0:8],
        "z": held.at[0:9, 0, 0, 0],
        "hop1": held.at[0:15, 0:2, 0, 0],
        "hop2": held.at[0:15, :, 0:2, 0],
        "up_down": held.at[0:3],
        "core": held.at[0:8],
    }

    def have_left(kind, part):
        described(part, part, along("z", 1), kind, ("label", 0)).wait_send()

    for stage, to in enumerate(([in_plane(o) for o in PLANE], column)):
        kind = ("plane", "column")[stage]
        sums[stage] = value
        for i, d in enumerate(to):
            copy(sums.at[stage], sums.at[base + i], d, kind, kind)
        if stage == 0:
            for sent, part in left.items():
                have_left(sent, part)
        arrived(sums.at[base : base + len(to)], kind)
        value = value + jnp.sum(sums[base : base + len(to)], axis=0)
        base += len(to)
    norms = jnp.sqrt(jnp.sum(value, axis=1, keepdims=True))
    trust = norms[0:1] / (norms[1:2] + 1e-06)
    trust_out[...] = jnp.broadcast_to(trust, trust_out.shape)
    have_left("plane", sums.at[0 : len(PLANE)])
    have_left("column", sums.at[0 : len(column)])


def finish(update, moment, second, trust, step_out, moment_out, second_out, scaled, done):
    copies = [
        pltpu.make_async_copy(moment, moment_out, done.at[0]),
        pltpu.make_async_copy(second, second_out, done.at[1]),
    ]
    for c in copies:
        c.start()
    n = ROWS // 4
    for i in range(4):
        at = pl.ds(i * n, n)
        scaled[at] = update[at] * trust[0:1, 0:1]
        copies.append(pltpu.make_async_copy(scaled.at[at], step_out.at[at], done.at[2 + i]))
        copies[-1].start()
    for c in copies:
        c.wait()


def shards(features, label_ids, label_count, weight, moment, second):
    hbm = pl.BlockSpec(memory_space=pltpu.HBM)
    vmem = pl.BlockSpec(memory_space=pltpu.VMEM)
    used = lax.broadcasted_iota(jnp.int32, label_ids.shape, 1) < label_count[:, None]
    ids = jnp.where(used, label_ids, -1)
    packed = jnp.concatenate([features.T.astype(jnp.float32), ids.T.astype(jnp.float32)], axis=0)
    f32, bf16, i32 = jnp.float32, jnp.bfloat16, jnp.int32
    block = jax.ShapeDtypeStruct(weight.shape, f32)
    results = pl.pallas_call(
        kernel,
        name="step",
        out_shape=(block, block, block, jax.ShapeDtypeStruct((8, 128), f32)),
        in_specs=[vmem, hbm, hbm, hbm],
        out_specs=(vmem, vmem, vmem, vmem),
        scratch_shapes=[
            pltpu.VMEM((4, 8, BLOCK_Q), i32),
            pltpu.VMEM(weight.shape, f32),
            pltpu.VMEM(weight.shape, f32),
            pltpu.VMEM(weight.shape, f32),
            pltpu.VMEM((2, ROWS, HALF), bf16),
            pltpu.VMEM((NZ, NY, NX, 2, BLOCK_D, BLOCK_Q), bf16),
            pltpu.VMEM((9, NY, NX, 8, BLOCK_Q), i32),
            pltpu.VMEM((8, NY, 8, BLOCK_Q), i32),
            pltpu.VMEM((2, ROWS, HALF), f32),
            pltpu.VMEM((48, 2, 128), f32),
            pltpu.SemaphoreType.DMA((len(KINDS),)),
            pltpu.SemaphoreType.DMA((N_ARRIVALS,)),
            pltpu.SemaphoreType.DMA((3,)),
        ],
        compiler_params=pltpu.CompilerParams(
            collective_id=0, has_side_effects=True, vmem_limit_bytes=411 << 17
        ),
    )(packed, weight, moment, second)
    return pl.pallas_call(
        finish,
        name="finish",
        out_shape=(block, block, block),
        in_specs=[vmem] * 4,
        out_specs=(hbm, hbm, hbm),
        scratch_shapes=[pltpu.VMEM(weight.shape, f32), pltpu.SemaphoreType.DMA((6,))],
        compiler_params=pltpu.CompilerParams(vmem_limit_bytes=8 << 20),
    )(*results)


def solution(mesh):
    in_specs = (
        P("dp", "label"),
        P("dp", None),
        P("dp"),
        P(("dp", "label"), None),
        P(("dp", "label"), None),
        P(("dp", "label"), None),
    )
    out_specs = (P(("dp", "label"), None), P(("dp", "label"), None), P(("dp", "label"), None))
    return jax.shard_map(shards, mesh=mesh, in_specs=in_specs, out_specs=out_specs, check_vma=False)
```

```python
import jax
import jax.numpy as jnp
from jax import lax
from jax.experimental import pallas as pl
from jax.experimental.pallas import tpu as pltpu
from jax.sharding import PartitionSpec as P

STEP = 10
MESH = pl.DeviceIdType.MESH
NX, NY, NZ = 4, 4, 16
WIDTH, ROWS, QUERIES = 768, 256, 4096
HALF = WIDTH // 2
BLOCK_D, BLOCK_Q = 48, 128
SCALE = 1.0 / WIDTH**0.5
LOG2_E = 1.4426950408889634
KINDS = ("label", "z", "hop1", "hop2", "up_down", "core", "plane", "column")
N_ARRIVALS = 58

GROUPS = {
    "own": (0, 1, "y"),
    "4": (4, 5, "x"),
    "12": (12, 13, "y"),
    "5": (5, 6, "x"),
    "11": (11, 12, "y"),
    "6": (6, 7, "x"),
    "10": (10, 11, "y"),
    "78": (7, 9, "x"),
    "9": (9, 10, "y"),
}
OTHERS = (1, 3, 2)
NEAR_Z = (4, 12, 3, 13, 2, 14, 1, 15)
FAR_Z = (8, 7, 9, 6, 10, 5, 11)
PLANE = sorted(
    ((i, j, k) for i in range(NX) for j in range(NY) for k in range(2) if i or j or k),
    key=lambda o: -(min(o[0], NX - o[0]) + min(o[1], NY - o[1]) + o[2]),
)

ORDER = (
    ("h1", "own"), ("h2", "own"), ("lab", 0), ("zh", 4), ("zh", 12), ("h1", "12"), ("h1", "4"),
    ("fz", 0, 0), ("lab", 1), ("h1", "11"), ("h2", "12"), ("h1", "5"), ("h3", "own"), ("h1", "6"),
    ("h1", "9"), ("h2", "4"), ("h1", "10"), ("h1", "78"), ("fz", 1, 0), ("greet",), ("lab", 2),
    ("h2", "9"), ("h2", "6"), ("fz", 0, 1), ("lab", 3), ("h2", "78"), ("h3", "4"), ("fz", 0, 2),
    ("h2", "10"), ("h3", "12"), ("fz", 0, 3), ("fz", 1, 1), ("p", 4), ("h3", "9"), ("h2", "11"),
    ("h3", "6"), ("fz", 1, 2), ("fz", 1, 3), ("h3", "10"), ("h2", "5"), ("fz", 2, 0), ("p", 1),
    ("fz", 2, 1), ("h3", "78"), ("p", 2), ("h3", "11"), ("p", 6), ("fz", 2, 2), ("fz", 2, 3),
    ("p", 7), ("h3", "5"), ("p", 0, 3, 5),
)


def kernel(
    packed, weight, moment, second,
    update_out, moment_out, second_out, trust_out,
    ids_t, w_in, mom_in, sec_in, w_bf, held, labels, words, acc, sums,
    send, recv, local,
):
    dp, lb = lax.axis_index("dp"), lax.axis_index("label")
    x, y, core = lax.rem(lb // 2, NX), lax.rem(dp, NY), lax.rem(lb, 2)
    z = (lb // 8) * 8 + dp // NY

    def device(x, y, z, core):
        return {"dp": lax.rem(z, 8) * NY + y, "label": (z // 8) * 8 + x * 2 + core}

    def along(axis, by):
        if axis == "x":
            return device(lax.rem(x + by, NX), y, z, core)
        if axis == "y":
            return device(x, lax.rem(y + by, NY), z, core)
        if axis == "z":
            return device(x, y, lax.rem(z + by, NZ), core)
        return device(x, y, z, 1 - core)

    def in_plane(offset):
        i, j, k = offset
        return device(lax.rem(x + i, NX), lax.rem(y + j, NY), z, lax.rem(core + k, 2))

    loads = {}
    for i, (name, src, dst) in enumerate(
        [
            ("weight", weight, w_in),
            ("moment", moment, mom_in),
            ("second", second, sec_in),
        ]
    ):
        loads[name] = pltpu.make_async_copy(src, dst, local.at[i])
        loads[name].start()

    barrier = pltpu.get_barrier_semaphore()
    def greet(devices):
        for to in devices:
            pl.semaphore_signal(barrier, inc=1, device_id=to, device_id_type=MESH)

    near = [along("z", by) for by in NEAR_Z]
    near += [in_plane(o) for o in PLANE if sum(1 for i in o if i) == 1]
    greet(near)
    later = [along("z", by) for by in FAR_Z]
    later += [in_plane(o) for o in PLANE if sum(1 for i in o if i) > 1]

    held[0, y, x, core] = packed[:BLOCK_D].astype(jnp.bfloat16)
    ids_t[...] = packed[BLOCK_D:].astype(jnp.int32).reshape(4, 8, BLOCK_Q)
    row, col = jnp.where(core == 0, y, x), jnp.where(core == 0, x, y)
    labels[3 + 5 * core, row, col] = ids_t[x]

    arrivals = {}

    def arrival(key):
        return recv.at[arrivals.setdefault(key, len(arrivals))]

    def described(src, dst, to, kind, key):
        return pltpu.make_async_remote_copy(
            src, dst, send.at[KINDS.index(kind)], arrival(key), device_id=to, device_id_type=MESH
        )

    def copy(src, dst, to, kind, key):
        described(src, dst, to, kind, key).start()

    def arrived(part, key):
        described(part, part, along("z", 1), "z", key).wait_recv()

    def blocks(n):
        if n <= NZ:
            return held.at[0:n, 0, 0, 0]
        return held.at[0 : n // 4, :, 0, 0] if n < 64 else held.at[0 : n // 32]

    pl.semaphore_wait(barrier, len(near))

    toward = 1 - 2 * core
    for k in (3, 2, 1, 0):
        to = device(x, y, lax.rem(z + toward * (k + 1) + NZ, NZ), core)
        there = 8 - core if k == 3 else (2 - k) * (1 - core) + (4 + k) * core
        copy(ids_t.at[x], labels.at[there, row, col], to, "label", ("label", 0))

    def label_hop(first, i):
        on_x = (core == 0) == first
        return device(
            jnp.where(on_x, lax.rem(x + i, NX), x), jnp.where(on_x, y, lax.rem(y + i, NY)), z, core
        )

    def slot(r):
        found = [n for n, (a, b, _) in GROUPS.items() if a <= r < b]
        return found[0] if found else "z" + str(min(r, NZ - r))

    def block(r):
        return held.at[r, y, x, core]

    for r in (4, 12):
        copy(block(0), block(r), along("z", NZ - r), "z", ("z", slot(r)))

    def hand_on(first):
        arrived(block(first), ("z", slot(first)))
        there = (8, 7, 6, 5) if first == 4 else (9, 10, 11)
        for r in there:
            by = (NZ + first - r) % NZ
            copy(block(first), block(r), along("z", by), "z", ("z", slot(r)))

    crossing = {}

    def hop1(name):
        a, b, axis = GROUPS[name]
        part = held.at[a:b, y, x, core]
        if name not in ("own", "4", "12"):
            arrived(part, ("z", name))
        for i in OTHERS:
            copy(part, part, along(axis, i), "hop1", ("hop1", name))

    def to_core(name, part, n):
        crossing[name] = crossing.get(name, 0) + n
        copy(part, part, along("core", 1), "core", ("core", name))

    def to_z(k, n, at):
        ups = held.at[(NZ - k) % NZ, :, at, core], held.at[NZ - 1 - k, :, at, core]
        downs = held.at[k, :, at, core], held.at[k + 1, :, at, core]
        copy(*ups, along("z", 1), "up_down", ("up_down", k, n))
        copy(*downs, along("z", NZ - 1), "up_down", ("up_down", k, n))

    def from_z(k, n):
        at = lax.rem(x + 4 - (0, *OTHERS)[n], 4)
        arrived(blocks(8), ("up_down", k, n))
        if k < 2:
            to_z(k + 1, n, at)
        for r in (k + 1, NZ - 1 - k):
            if k == 2:
                to_core("z3", held.at[r, :, at, core], 4)
            elif n == 3:
                to_core("z" + str(k + 1), held.at[r, :, :, core], 16)

    def hop2(name):
        a, b, axis = GROUPS[name]
        arrived(blocks(3 * (b - a)), ("hop1", name))
        part = held.at[a:b, y, :, core] if axis == "x" else held.at[a:b, :, x, core]
        for n, i in enumerate(OTHERS):
            key = ("hop2", name, n) if name == "own" else ("hop2", name)
            copy(part, part, along("y" if axis == "x" else "x", i), "hop2", key)
        if name == "own":
            to_z(0, 0, x)

    def hop3(name):
        a, b, _ = GROUPS[name]
        if name == "own":
            for n, i in enumerate(OTHERS):
                arrived(blocks(4), ("hop2", name, n))
                to_z(0, n + 1, lax.rem(x + 4 - i, 4))
        else:
            arrived(blocks(12 * (b - a)), ("hop2", name))
        for r in range(a, b):
            to_core(name, held.at[r, :, :, core], 16)

    waiting = set()

    def done(name):
        if name not in waiting:
            waiting.add(name)
            arrived(blocks(crossing[name]), ("core", name))

    first = (dp * 16 + lb) * ROWS

    def mark(i, core):
        pos, at = i // NY, lax.rem(i, NY)
        if core == 0:
            pair, found = lax.rem(pos + 5, 8), labels[pos, at]
        else:
            pair, found = pos + 1, labels[4 + pos, :, at]
        local_id = found - first
        word = local_id >> 5
        bit = jnp.left_shift(jnp.int32(1), local_id & 31)
        rows = lax.broadcasted_iota(jnp.int32, (8, BLOCK_Q), 0)
        out = jnp.zeros((8, BLOCK_Q), jnp.int32)
        for w in range(8):
            hit = jnp.where(word == w, bit, 0)
            hit = (hit[0] | hit[1]) | (hit[2] | hit[3])
            for by in (4, 2, 1):
                hit = hit | pltpu.roll(hit, by, 0)
            out = jnp.where(rows == w, hit, out)
        words[pair, at] = out
        return core

    def label(stage):
        part = labels.at[0 : (0, 0, 3, 4)[stage]] if stage > 1 else labels.at[0 : 4 - stage, 0]
        arrived(part if stage else labels.at[0:4, 0, 0], ("label", stage))
        if stage == 3:
            for i in range(2):
                lax.fori_loop(0, 4 * NY, lambda n, _, i=i: (mark(n, i), 0)[1], 0)
            return
        mine = labels.at[pl.ds(4 * core, 4)]
        part = (mine.at[:, row, col], mine.at[:, row], mine)[stage]
        to = [label_hop(stage == 0, i) for i in OTHERS] if stage < 2 else [along("core", 1)]
        for d in to:
            copy(part, part, d, "label", ("label", stage + 1))

    def pair(r):
        lo = lax.rem(z + r, NZ) // 8
        q = NY * BLOCK_Q

        def slab(at):
            return jnp.concatenate([held[at, i].reshape(HALF, BLOCK_Q) for i in range(NY)], axis=1)

        rows = jnp.concatenate([slab(r), slab(r + 8)], axis=0)
        both = jnp.concatenate([w_bf[lo], w_bf[1 - lo]], axis=1)
        scores = jnp.dot(both, rows, preferred_element_type=jnp.float32)
        prob = 1.0 / (1.0 + jnp.exp2(scores * (-SCALE * LOG2_E)))
        marks = jnp.concatenate([words[r, i] for i in range(NY)], axis=1)
        bits = jnp.left_shift(jnp.int32(1), lax.broadcasted_iota(jnp.int32, (32, q), 0))
        target = jnp.concatenate(
            [(jnp.broadcast_to(marks[w : w + 1], (32, q)) & bits) != 0 for w in range(8)], axis=0
        )
        dscore = (prob - jnp.where(target, 1.0, 0.0)).astype(jnp.bfloat16)
        dims = (((1,), (1,)), ((), ()))
        g = lax.dot_general(dscore, rows, dims, preferred_element_type=jnp.float32)
        acc[lo] += g[:, :HALF]
        acc[1 - lo] += g[:, HALF:]

    steps = {"zh": hand_on, "h1": hop1, "h2": hop2, "h3": hop3, "fz": from_z, "lab": label}
    for at, (what, *args) in enumerate(ORDER):
        if at == 2:
            loads["weight"].wait()
            w_bf[0] = w_in[:, :HALF].astype(jnp.bfloat16)
            w_bf[1] = w_in[:, HALF:].astype(jnp.bfloat16)
            acc[...] = jnp.zeros_like(acc)
        if what == "greet":
            done("own")
            greet(later)
            continue
        if what != "p":
            steps[what](*args)
            continue
        for r in args:
            done(slot(r))
            done(slot(r + 8))
        for r in args:
            pair(r)

    loads["moment"].wait()
    loads["second"].wait()
    step_rows = 32

    def refresh(i, carry):
        at = pl.ds(pl.multiple_of(i * step_rows, step_rows), step_rows)
        totals = list(carry)
        for h in range(2):
            cols = slice(h * HALF, (h + 1) * HALF)
            g = acc[h, at] * (SCALE / QUERIES)
            w = w_in[at, cols]
            m = 0.9 * mom_in[at, cols] + 0.1 * g
            v = 0.999 * sec_in[at, cols] + 0.001 * g * g
            u = (m * (1.0 / (1.0 - 0.9**STEP))) / (
                jnp.sqrt(v * (1.0 / (1.0 - 0.999**STEP))) + 1e-06
            ) + 0.01 * w
            update_out[at, cols] = u
            moment_out[at, cols] = m
            second_out[at, cols] = v
            for k, s in enumerate((w * w, u * u)):
                s = jnp.sum(s.reshape(step_rows // 8, 8, HALF), axis=0)
                totals[k] += s[:, :128] + s[:, 128:256] + s[:, 256:]
        return tuple(totals)

    zero = jnp.zeros((8, 128), jnp.float32)
    totals = lax.fori_loop(0, ROWS // step_rows, refresh, (zero, zero))
    value = jnp.concatenate([jnp.sum(t, axis=0, keepdims=True) for t in totals], axis=0)

    pl.semaphore_wait(barrier, len(later))
    base = 2
    column = [along("z", by) for by in (*FAR_Z, *NEAR_Z)]
    left = {
        "label": labels.at[0:8],
        "z": held.at[0:9, 0, 0, 0],
        "hop1": held.at[0:15, 0:2, 0, 0],
        "hop2": held.at[0:15, :, 0:2, 0],
        "up_down": held.at[0:3],
        "core": held.at[0:8],
    }

    def have_left(kind, part):
        described(part, part, along("z", 1), kind, ("label", 0)).wait_send()

    for stage, to in enumerate(([in_plane(o) for o in PLANE], column)):
        kind = ("plane", "column")[stage]
        sums[stage] = value
        for i, d in enumerate(to):
            copy(sums.at[stage], sums.at[base + i], d, kind, kind)
        if stage == 0:
            for sent, part in left.items():
                have_left(sent, part)
        arrived(sums.at[base : base + len(to)], kind)
        value = value + jnp.sum(sums[base : base + len(to)], axis=0)
        base += len(to)
    norms = jnp.sqrt(jnp.sum(value, axis=1, keepdims=True))
    trust = norms[0:1] / (norms[1:2] + 1e-06)
    trust_out[...] = jnp.broadcast_to(trust, trust_out.shape)
    have_left("plane", sums.at[0 : len(PLANE)])
    have_left("column", sums.at[0 : len(column)])


def finish(update, moment, second, trust, step_out, moment_out, second_out, scaled, done):
    copies = [
        pltpu.make_async_copy(moment, moment_out, done.at[0]),
        pltpu.make_async_copy(second, second_out, done.at[1]),
    ]
    for c in copies:
        c.start()
    n = ROWS // 4
    for i in range(4):
        at = pl.ds(i * n, n)
        scaled[at] = update[at] * trust[0:1, 0:1]
        copies.append(pltpu.make_async_copy(scaled.at[at], step_out.at[at], done.at[2 + i]))
        copies[-1].start()
    for c in copies:
        c.wait()


def shards(features, label_ids, label_count, weight, moment, second):
    hbm = pl.BlockSpec(memory_space=pltpu.HBM)
    vmem = pl.BlockSpec(memory_space=pltpu.VMEM)
    used = lax.broadcasted_iota(jnp.int32, label_ids.shape, 1) < label_count[:, None]
    ids = jnp.where(used, label_ids, -1)
    packed = jnp.concatenate([features.T.astype(jnp.float32), ids.T.astype(jnp.float32)], axis=0)
    f32, bf16, i32 = jnp.float32, jnp.bfloat16, jnp.int32
    block = jax.ShapeDtypeStruct(weight.shape, f32)
    results = pl.pallas_call(
        kernel,
        name="step",
        out_shape=(block, block, block, jax.ShapeDtypeStruct((8, 128), f32)),
        in_specs=[vmem, hbm, hbm, hbm],
        out_specs=(vmem, vmem, vmem, vmem),
        scratch_shapes=[
            pltpu.VMEM((4, 8, BLOCK_Q), i32),
            pltpu.VMEM(weight.shape, f32),
            pltpu.VMEM(weight.shape, f32),
            pltpu.VMEM(weight.shape, f32),
            pltpu.VMEM((2, ROWS, HALF), bf16),
            pltpu.VMEM((NZ, NY, NX, 2, BLOCK_D, BLOCK_Q), bf16),
            pltpu.VMEM((9, NY, NX, 8, BLOCK_Q), i32),
            pltpu.VMEM((8, NY, 8, BLOCK_Q), i32),
            pltpu.VMEM((2, ROWS, HALF), f32),
            pltpu.VMEM((48, 2, 128), f32),
            pltpu.SemaphoreType.DMA((len(KINDS),)),
            pltpu.SemaphoreType.DMA((N_ARRIVALS,)),
            pltpu.SemaphoreType.DMA((3,)),
        ],
        compiler_params=pltpu.CompilerParams(
            collective_id=0, has_side_effects=True, vmem_limit_bytes=411 << 17
        ),
    )(packed, weight, moment, second)
    return pl.pallas_call(
        finish,
        name="finish",
        out_shape=(block, block, block),
        in_specs=[vmem] * 4,
        out_specs=(hbm, hbm, hbm),
        scratch_shapes=[pltpu.VMEM(weight.shape, f32), pltpu.SemaphoreType.DMA((6,))],
        compiler_params=pltpu.CompilerParams(vmem_limit_bytes=8 << 20),
    )(*results)


def solution(mesh):
    in_specs = (
        P("dp", "label"),
        P("dp", None),
        P("dp"),
        P(("dp", "label"), None),
        P(("dp", "label"), None),
        P(("dp", "label"), None),
    )
    out_specs = (P(("dp", "label"), None), P(("dp", "label"), None), P(("dp", "label"), None))
    return jax.shard_map(shards, mesh=mesh, in_specs=in_specs, out_specs=out_specs, check_vma=False)
```

```python
import jax
import jax.numpy as jnp
from jax import lax
from jax.experimental import pallas as pl
from jax.experimental.pallas import tpu as pltpu
from jax.sharding import PartitionSpec as P

STEP = 10
MESH = pl.DeviceIdType.MESH
NX, NY, NZ = 4, 4, 16
WIDTH, ROWS, QUERIES = 768, 256, 4096
HALF = WIDTH // 2
BLOCK_D, BLOCK_Q = 48, 128
SCALE = 1.0 / WIDTH**0.5
LOG2_E = 1.4426950408889634
KINDS = ("label", "z", "hop1", "hop2", "up_down", "core", "plane", "column")
N_ARRIVALS = 58

GROUPS = {
    "own": (0, 1, "y"),
    "4": (4, 5, "x"),
    "12": (12, 13, "y"),
    "5": (5, 6, "x"),
    "11": (11, 12, "y"),
    "6": (6, 7, "x"),
    "10": (10, 11, "y"),
    "78": (7, 9, "x"),
    "9": (9, 10, "y"),
}
OTHERS = (1, 3, 2)
NEAR_Z = (4, 12, 3, 13, 2, 14, 1, 15)
FAR_Z = (8, 7, 9, 6, 10, 5, 11)
PLANE = sorted(
    ((i, j, k) for i in range(NX) for j in range(NY) for k in range(2) if i or j or k),
    key=lambda o: -(min(o[0], NX - o[0]) + min(o[1], NY - o[1]) + o[2]),
)

ORDER = (
    ("h1", "own"), ("h2", "own"), ("lab", 0), ("zh", 4), ("zh", 12), ("h1", "4"), ("h1", "12"),
    ("fz", 0, 0), ("lab", 1), ("h1", "11"), ("h1", "5"), ("h2", "12"), ("h3", "own"), ("h1", "9"),
    ("h1", "6"), ("h2", "4"), ("h1", "10"), ("h1", "78"), ("fz", 1, 0), ("h2", "11"), ("greet",), ("lab", 2),
    ("h2", "9"), ("h2", "6"), ("fz", 0, 1), ("fz", 0, 2), ("fz", 0, 3), ("lab", 3), ("h2", "78"),
    ("fz", 2, 0), ("h2", "10"), ("h3", "4"), ("h3", "12"), ("h3", "6"), ("fz", 1, 1), ("p", 4),
    ("fz", 1, 2), ("fz", 1, 3), ("h2", "5"), ("h3", "11"), ("h3", "9"), ("h3", "10"), ("p", 6),
    ("h3", "78"), ("fz", 2, 1), ("p", 1, 2), ("fz", 2, 2), ("fz", 2, 3), ("h3", "5"),
    ("p", 0, 7, 3), ("p", 5),
)


def kernel(
    packed, weight, moment, second,
    update_out, moment_out, second_out, trust_out,
    ids_t, w_in, mom_in, sec_in, w_bf, held, labels, words, acc, sums,
    send, recv, local,
):
    dp, lb = lax.axis_index("dp"), lax.axis_index("label")
    x, y, core = lax.rem(lb // 2, NX), lax.rem(dp, NY), lax.rem(lb, 2)
    z = (lb // 8) * 8 + dp // NY

    def device(x, y, z, core):
        return {"dp": lax.rem(z, 8) * NY + y, "label": (z // 8) * 8 + x * 2 + core}

    def along(axis, by):
        if axis == "x":
            return device(lax.rem(x + by, NX), y, z, core)
        if axis == "y":
            return device(x, lax.rem(y + by, NY), z, core)
        if axis == "z":
            return device(x, y, lax.rem(z + by, NZ), core)
        return device(x, y, z, 1 - core)

    def in_plane(offset):
        i, j, k = offset
        return device(lax.rem(x + i, NX), lax.rem(y + j, NY), z, lax.rem(core + k, 2))

    loads = {}
    for i, (name, src, dst) in enumerate(
        [
            ("weight", weight, w_in),
            ("moment", moment, mom_in),
            ("second", second, sec_in),
        ]
    ):
        loads[name] = pltpu.make_async_copy(src, dst, local.at[i])
        loads[name].start()

    barrier = pltpu.get_barrier_semaphore()
    def greet(devices):
        for to in devices:
            pl.semaphore_signal(barrier, inc=1, device_id=to, device_id_type=MESH)

    near = [along("z", by) for by in NEAR_Z]
    near += [in_plane(o) for o in PLANE if sum(1 for i in o if i) == 1]
    greet(near)
    later = [along("z", by) for by in FAR_Z]
    later += [in_plane(o) for o in PLANE if sum(1 for i in o if i) > 1]

    held[0, y, x, core] = packed[:BLOCK_D].astype(jnp.bfloat16)
    ids_t[...] = packed[BLOCK_D:].astype(jnp.int32).reshape(4, 8, BLOCK_Q)
    row, col = jnp.where(core == 0, y, x), jnp.where(core == 0, x, y)
    labels[3 + 5 * core, row, col] = ids_t[x]

    arrivals = {}

    def arrival(key):
        return recv.at[arrivals.setdefault(key, len(arrivals))]

    def described(src, dst, to, kind, key):
        return pltpu.make_async_remote_copy(
            src, dst, send.at[KINDS.index(kind)], arrival(key), device_id=to, device_id_type=MESH
        )

    def copy(src, dst, to, kind, key):
        described(src, dst, to, kind, key).start()

    def arrived(part, key):
        described(part, part, along("z", 1), "z", key).wait_recv()

    def blocks(n):
        if n <= NZ:
            return held.at[0:n, 0, 0, 0]
        return held.at[0 : n // 4, :, 0, 0] if n < 64 else held.at[0 : n // 32]

    pl.semaphore_wait(barrier, len(near))

    def label_hop(first, i):
        on_x = (core == 0) == first
        return device(
            jnp.where(on_x, lax.rem(x + i, NX), x), jnp.where(on_x, y, lax.rem(y + i, NY)), z, core
        )

    def slot(r):
        found = [n for n, (a, b, _) in GROUPS.items() if a <= r < b]
        return found[0] if found else "z" + str(min(r, NZ - r))

    def block(r):
        return held.at[r, y, x, core]

    for r in (4, 12):
        copy(block(0), block(r), along("z", NZ - r), "z", ("z", slot(r)))

    toward = 1 - 2 * core
    for k in (3, 2, 1, 0):
        to = device(x, y, lax.rem(z + toward * (k + 1) + NZ, NZ), core)
        there = 8 - core if k == 3 else (2 - k) * (1 - core) + (4 + k) * core
        copy(ids_t.at[x], labels.at[there, row, col], to, "label", ("label", 0))

    def hand_on(first):
        arrived(block(first), ("z", slot(first)))
        there = (8, 7, 6, 5) if first == 4 else (9, 10, 11)
        for r in there:
            by = (NZ + first - r) % NZ
            copy(block(first), block(r), along("z", by), "z", ("z", slot(r)))

    crossing = {}

    def hop1(name):
        a, b, axis = GROUPS[name]
        part = held.at[a:b, y, x, core]
        if name not in ("own", "4", "12"):
            arrived(part, ("z", name))
        for i in OTHERS:
            copy(part, part, along(axis, i), "hop1", ("hop1", name))

    def to_core(name, part, n):
        crossing[name] = crossing.get(name, 0) + n
        copy(part, part, along("core", 1), "core", ("core", name))

    def to_z(k, n, at):
        ups = held.at[(NZ - k) % NZ, :, at, core], held.at[NZ - 1 - k, :, at, core]
        downs = held.at[k, :, at, core], held.at[k + 1, :, at, core]
        copy(*ups, along("z", 1), "up_down", ("up_down", k, n))
        copy(*downs, along("z", NZ - 1), "up_down", ("up_down", k, n))

    def from_z(k, n):
        at = lax.rem(x + 4 - (0, *OTHERS)[n], 4)
        arrived(blocks(8), ("up_down", k, n))
        if k < 2:
            to_z(k + 1, n, at)
        for r in (k + 1, NZ - 1 - k):
            if k == 2:
                to_core("z3", held.at[r, :, at, core], 4)
            elif n == 3:
                to_core("z" + str(k + 1), held.at[r, :, :, core], 16)

    def hop2(name):
        a, b, axis = GROUPS[name]
        arrived(blocks(3 * (b - a)), ("hop1", name))
        part = held.at[a:b, y, :, core] if axis == "x" else held.at[a:b, :, x, core]
        for n, i in enumerate(OTHERS):
            key = ("hop2", name, n) if name == "own" else ("hop2", name)
            copy(part, part, along("y" if axis == "x" else "x", i), "hop2", key)
        if name == "own":
            to_z(0, 0, x)

    def hop3(name):
        a, b, _ = GROUPS[name]
        if name == "own":
            for n, i in enumerate(OTHERS):
                arrived(blocks(4), ("hop2", name, n))
                to_z(0, n + 1, lax.rem(x + 4 - i, 4))
        else:
            arrived(blocks(12 * (b - a)), ("hop2", name))
        for r in range(a, b):
            to_core(name, held.at[r, :, :, core], 16)

    waiting = set()

    def done(name):
        if name not in waiting:
            waiting.add(name)
            arrived(blocks(crossing[name]), ("core", name))

    first = (dp * 16 + lb) * ROWS

    def mark(i, core):
        pos, at = i // NY, lax.rem(i, NY)
        if core == 0:
            pair, found = lax.rem(pos + 5, 8), labels[pos, at]
        else:
            pair, found = pos + 1, labels[4 + pos, :, at]
        local_id = found - first
        word = local_id >> 5
        bit = jnp.left_shift(jnp.int32(1), local_id & 31)
        rows = lax.broadcasted_iota(jnp.int32, (8, BLOCK_Q), 0)
        out = jnp.zeros((8, BLOCK_Q), jnp.int32)
        for w in range(8):
            hit = jnp.where(word == w, bit, 0)
            hit = (hit[0] | hit[1]) | (hit[2] | hit[3])
            for by in (4, 2, 1):
                hit = hit | pltpu.roll(hit, by, 0)
            out = jnp.where(rows == w, hit, out)
        words[pair, at] = out
        return core

    def label(stage):
        part = labels.at[0 : (0, 0, 3, 4)[stage]] if stage > 1 else labels.at[0 : 4 - stage, 0]
        arrived(part if stage else labels.at[0:4, 0, 0], ("label", stage))
        if stage == 3:
            for i in range(2):
                lax.fori_loop(0, 4 * NY, lambda n, _, i=i: (mark(n, i), 0)[1], 0)
            return
        mine = labels.at[pl.ds(4 * core, 4)]
        part = (mine.at[:, row, col], mine.at[:, row], mine)[stage]
        to = [label_hop(stage == 0, i) for i in OTHERS] if stage < 2 else [along("core", 1)]
        for d in to:
            copy(part, part, d, "label", ("label", stage + 1))

    def pair(r):
        lo = lax.rem(z + r, NZ) // 8
        q = NY * BLOCK_Q

        def slab(at):
            return jnp.concatenate([held[at, i].reshape(HALF, BLOCK_Q) for i in range(NY)], axis=1)

        rows = jnp.concatenate([slab(r), slab(r + 8)], axis=0)
        both = jnp.concatenate([w_bf[lo], w_bf[1 - lo]], axis=1)
        scores = jnp.dot(both, rows, preferred_element_type=jnp.float32)
        prob = 1.0 / (1.0 + jnp.exp2(scores * (-SCALE * LOG2_E)))
        marks = jnp.concatenate([words[r, i] for i in range(NY)], axis=1)
        bits = jnp.left_shift(jnp.int32(1), lax.broadcasted_iota(jnp.int32, (32, q), 0))
        target = jnp.concatenate(
            [(jnp.broadcast_to(marks[w : w + 1], (32, q)) & bits) != 0 for w in range(8)], axis=0
        )
        dscore = (prob - jnp.where(target, 1.0, 0.0)).astype(jnp.bfloat16)
        dims = (((1,), (1,)), ((), ()))
        g = lax.dot_general(dscore, rows, dims, preferred_element_type=jnp.float32)
        acc[lo] += g[:, :HALF]
        acc[1 - lo] += g[:, HALF:]

    steps = {"zh": hand_on, "h1": hop1, "h2": hop2, "h3": hop3, "fz": from_z, "lab": label}
    for at, (what, *args) in enumerate(ORDER):
        if at == 2:
            loads["weight"].wait()
            w_bf[0] = w_in[:, :HALF].astype(jnp.bfloat16)
            w_bf[1] = w_in[:, HALF:].astype(jnp.bfloat16)
            acc[...] = jnp.zeros_like(acc)
        if what == "greet":
            done("own")
            greet(later)
            continue
        if what != "p":
            steps[what](*args)
            continue
        for r in args:
            done(slot(r))
            done(slot(r + 8))
        for r in args:
            pair(r)

    loads["moment"].wait()
    loads["second"].wait()
    step_rows = 32

    def refresh(i, carry):
        at = pl.ds(pl.multiple_of(i * step_rows, step_rows), step_rows)
        totals = list(carry)
        for h in range(2):
            cols = slice(h * HALF, (h + 1) * HALF)
            g = acc[h, at] * (SCALE / QUERIES)
            w = w_in[at, cols]
            m = 0.9 * mom_in[at, cols] + 0.1 * g
            v = 0.999 * sec_in[at, cols] + 0.001 * g * g
            u = (m * (1.0 / (1.0 - 0.9**STEP))) / (
                jnp.sqrt(v * (1.0 / (1.0 - 0.999**STEP))) + 1e-06
            ) + 0.01 * w
            update_out[at, cols] = u
            moment_out[at, cols] = m
            second_out[at, cols] = v
            for k, s in enumerate((w * w, u * u)):
                s = jnp.sum(s.reshape(step_rows // 8, 8, HALF), axis=0)
                totals[k] += s[:, :128] + s[:, 128:256] + s[:, 256:]
        return tuple(totals)

    zero = jnp.zeros((8, 128), jnp.float32)
    totals = lax.fori_loop(0, ROWS // step_rows, refresh, (zero, zero))
    value = jnp.concatenate([jnp.sum(t, axis=0, keepdims=True) for t in totals], axis=0)

    pl.semaphore_wait(barrier, len(later))
    base = 2
    column = [along("z", by) for by in (*FAR_Z, *NEAR_Z)]
    left = {
        "label": labels.at[0:8],
        "z": held.at[0:9, 0, 0, 0],
        "hop1": held.at[0:15, 0:2, 0, 0],
        "hop2": held.at[0:15, :, 0:2, 0],
        "up_down": held.at[0:3],
        "core": held.at[0:8],
    }

    def have_left(kind, part):
        described(part, part, along("z", 1), kind, ("label", 0)).wait_send()

    for stage, to in enumerate(([in_plane(o) for o in PLANE], column)):
        kind = ("plane", "column")[stage]
        sums[stage] = value
        for i, d in enumerate(to):
            copy(sums.at[stage], sums.at[base + i], d, kind, kind)
        if stage == 0:
            for sent, part in left.items():
                have_left(sent, part)
        arrived(sums.at[base : base + len(to)], kind)
        value = value + jnp.sum(sums[base : base + len(to)], axis=0)
        base += len(to)
    norms = jnp.sqrt(jnp.sum(value, axis=1, keepdims=True))
    trust = norms[0:1] / (norms[1:2] + 1e-06)
    trust_out[...] = jnp.broadcast_to(trust, trust_out.shape)
    have_left("plane", sums.at[0 : len(PLANE)])
    have_left("column", sums.at[0 : len(column)])


def finish(update, moment, second, trust, step_out, moment_out, second_out, scaled, done):
    copies = [
        pltpu.make_async_copy(moment, moment_out, done.at[0]),
        pltpu.make_async_copy(second, second_out, done.at[1]),
    ]
    for c in copies:
        c.start()
    n = ROWS // 4
    for i in range(4):
        at = pl.ds(i * n, n)
        scaled[at] = update[at] * trust[0:1, 0:1]
        copies.append(pltpu.make_async_copy(scaled.at[at], step_out.at[at], done.at[2 + i]))
        copies[-1].start()
    for c in copies:
        c.wait()


def shards(features, label_ids, label_count, weight, moment, second):
    hbm = pl.BlockSpec(memory_space=pltpu.HBM)
    vmem = pl.BlockSpec(memory_space=pltpu.VMEM)
    used = lax.broadcasted_iota(jnp.int32, label_ids.shape, 1) < label_count[:, None]
    ids = jnp.where(used, label_ids, -1)
    packed = jnp.concatenate([features.T.astype(jnp.float32), ids.T.astype(jnp.float32)], axis=0)
    f32, bf16, i32 = jnp.float32, jnp.bfloat16, jnp.int32
    block = jax.ShapeDtypeStruct(weight.shape, f32)
    results = pl.pallas_call(
        kernel,
        name="step",
        out_shape=(block, block, block, jax.ShapeDtypeStruct((8, 128), f32)),
        in_specs=[vmem, hbm, hbm, hbm],
        out_specs=(vmem, vmem, vmem, vmem),
        scratch_shapes=[
            pltpu.VMEM((4, 8, BLOCK_Q), i32),
            pltpu.VMEM(weight.shape, f32),
            pltpu.VMEM(weight.shape, f32),
            pltpu.VMEM(weight.shape, f32),
            pltpu.VMEM((2, ROWS, HALF), bf16),
            pltpu.VMEM((NZ, NY, NX, 2, BLOCK_D, BLOCK_Q), bf16),
            pltpu.VMEM((9, NY, NX, 8, BLOCK_Q), i32),
            pltpu.VMEM((8, NY, 8, BLOCK_Q), i32),
            pltpu.VMEM((2, ROWS, HALF), f32),
            pltpu.VMEM((48, 2, 128), f32),
            pltpu.SemaphoreType.DMA((len(KINDS),)),
            pltpu.SemaphoreType.DMA((N_ARRIVALS,)),
            pltpu.SemaphoreType.DMA((3,)),
        ],
        compiler_params=pltpu.CompilerParams(
            collective_id=0, has_side_effects=True, vmem_limit_bytes=411 << 17
        ),
    )(packed, weight, moment, second)
    return pl.pallas_call(
        finish,
        name="finish",
        out_shape=(block, block, block),
        in_specs=[vmem] * 4,
        out_specs=(hbm, hbm, hbm),
        scratch_shapes=[pltpu.VMEM(weight.shape, f32), pltpu.SemaphoreType.DMA((6,))],
        compiler_params=pltpu.CompilerParams(vmem_limit_bytes=8 << 20),
    )(*results)


def solution(mesh):
    in_specs = (
        P("dp", "label"),
        P("dp", None),
        P("dp"),
        P(("dp", "label"), None),
        P(("dp", "label"), None),
        P(("dp", "label"), None),
    )
    out_specs = (P(("dp", "label"), None), P(("dp", "label"), None), P(("dp", "label"), None))
    return jax.shard_map(shards, mesh=mesh, in_specs=in_specs, out_specs=out_specs, check_vma=False)
```
